512 devices in a mesh: expert: 32 (over x_lo, z), tensor: 16 (over y, x_hi, core).
Axes of the slice: x: 4 (x_hi: 2, x_lo: 2; x = x_hi * 2 + x_lo), y: 4, z: 16, core: 2. Of those that a mesh axis runs over, the one named last changes fastest.
Arguments:
- tokens: bfloat16 [1536, 5120], P('expert', 'tensor'), may hold values from -6 to 6
- expert_ids: int32 [1536, 6], P('expert'), may hold values from 0 to 31, all different within a row; in each aligned block of 48 rows (0 to 47, 48 to 95, ...) at most 18 rows name the same one
- route_weights: float32 [1536, 6], P('expert'), may hold values from 0.05 to 0.6
- routed_gate: bfloat16 [32, 1536, 5120], P('expert', 'tensor'), may hold values from -0.078125 to 0.078125
- routed_up: bfloat16 [32, 1536, 5120], P('expert', 'tensor'), may hold values from -0.078125 to 0.078125
- routed_down: bfloat16 [32, 1536, 5120], P('expert', None, 'tensor'), may hold values from -0.15625 to 0.15625
- shared_gate: bfloat16 [5120, 3072], P('expert', 'tensor'), may hold values from -0.078125 to 0.078125
- shared_up: bfloat16 [5120, 3072], P('expert', 'tensor'), may hold values from -0.078125 to 0.078125
- shared_down: bfloat16 [3072, 5120], P('tensor', 'expert'), may hold values from -0.21875 to 0.21875
- norm_gain: float32 [5120], replicated, may hold values from 0.25 to 1.75
- proj_weight: bfloat16 [2112, 5120], P('tensor'), may hold values from -0.078125 to 0.078125
Outputs:
- stream: bfloat16 [1536, 5120], P('expert', 'tensor')
- projected: bfloat16 [1536, 2112], P('expert', 'tensor')
The draws below stay inside these ranges and needn't reach their ends.
Inputs may be any that keep to these rules, and one draw needn't show every extreme that they name: `expert_ids`: in each aligned block of 48 tokens (those of one index of expert) no expert is chosen by more than 18 tokens, and some expert is chosen by exactly 18; a token's 6 experts differ.
All inputs are finite; a program needn't handle non-finite values.
Results may differ from the reference program's by a relative error of at most 0.019.
Values may be sent and summed in bfloat16 or wider, within the bound.
No kernel may reach another device: no remote copies, remote signals or barrier semaphores. Data moves between devices by JAX's collectives and lax.ppermute only.
A program may use at most 128 MiB of HBM per device.

```python
import math
import jax
import jax.numpy as jnp
import numpy as np
from jax import lax

D = 5120
HID = 1536
SH = 3072
TOP = 6
QA = 1536
KVA = 576
TOK_DEV = 48
EXPERTS = 32
TOKENS = 1536
CAP = 18


def raised(drawn, key, source, target, blocks, factor):
    owner, partner = [(jnp.arange(drawn.shape[dim]) // (drawn.shape[dim] // blocks)).reshape([-1 if axis == dim else 1 for axis in range(drawn.ndim)]) for dim in (source, target)]
    chosen = jax.random.permutation(key, blocks)[partner]
    strong = (owner == chosen) | (owner == (partner + blocks // 2) % blocks)
    return jnp.where(strong, factor * drawn, drawn)


def level_of(key, extent, cuts, low, largest):
    gain = 1.0
    for position, parts in cuts:
        steps = jax.random.uniform(jax.random.fold_in(jax.random.fold_in(key, 6), position), (parts,), jnp.float32, low / len(cuts), largest / len(cuts))
        gain = gain * jnp.repeat(jnp.exp(steps), extent[position] // parts).reshape((-1,) + (1,) * (len(extent) - 1 - position))
    return gain


def assign_block(rng, own, number, rows, amount, top, bound, slope):
    sequence = jax.random.permutation(rng, amount)
    crowded, common = portions_of(amount, rows * top, bound, slope, True), portions_of(amount, rows * top, bound, slope, False)
    places = jnp.arange(amount)

    def named(sizes, offset_by):
        used = int((sizes > 0).sum())
        fixed = max(1, used // 4)
        shifted = fixed + (places - fixed + offset_by * (used - fixed)) % max(1, amount - fixed)
        return jnp.zeros((amount,), jnp.int32).at[sequence[jnp.where(places < fixed, places, shifted)]].set(jnp.asarray(sizes, jnp.int32))

    sizes = jnp.where(number % 4 == 0, named(crowded, number // 4), named(common, number - number // 4 - 1))
    mixed = jax.random.permutation(jax.random.fold_in(own, 3), amount)
    donor, receiver = mixed[0:amount // 2 * 2:2], mixed[1:amount // 2 * 2:2]
    margin = jnp.minimum(sizes[donor] - 1, bound - sizes[receiver]) // 2
    margin = jnp.where((donor == sequence[0]) | (receiver == sequence[0]) | (sizes[receiver] == 0), 0, jnp.maximum(margin, 0))
    shifted = jax.random.randint(jax.random.fold_in(own, 4), (amount // 2,), 0, 1 << 20) % (margin + 1)
    sizes = sizes.at[donor].add(-shifted).at[receiver].add(shifted)
    labels = jnp.searchsorted(jnp.cumsum(sizes), jnp.arange(rows * top), side="right").astype(jnp.int32)
    listing = labels.reshape(top, rows).T
    listing = listing[jax.random.permutation(jax.random.fold_in(own, 1), rows)]
    offset_by = jax.random.randint(jax.random.fold_in(own, 2), (rows, 1), 0, top)
    return jnp.take_along_axis(listing, (jnp.arange(top)[None, :] + offset_by) % top, axis=1)


def portions_of(number_of, total, reach, skew, full):
    portions = [(1 << 20) // math.isqrt(grade ** skew) + 1 for grade in range(1, number_of + 1)]
    largest = reach if full else min(reach, max(-(-total // number_of), total * portions[0] // sum(portions)))
    least = 1 if total - largest >= number_of - 1 else 0
    given, rest = [largest] + [least] * (number_of - 1), total - largest - least * (number_of - 1)
    while rest > 0:
        movable = [i for i in range(1, number_of) if given[i] < largest] or [i for i in range(1, number_of) if given[i] < reach]
        whole, remaining = sum([portions[i] for i in movable]), rest
        for i in movable:
            more = min(reach - given[i], max(1, remaining * portions[i] // whole), rest)
            given[i] = given[i] + more
            rest = rest - more
    return np.array(given)


def normal_values(rng, dims, spread, most, shards=(), kind=jnp.bfloat16):
    loudness = level_of(rng, dims, shards, -0.22, 0.18) if shards else 1.0
    drawn = jax.random.normal(rng, dims, jnp.float32) * spread * loudness
    return jnp.minimum(jnp.maximum(drawn, -most), most).astype(kind)


def heavy_noise(own_key, extent, spread, reach, split, heavy, held_as=jnp.bfloat16):
    values = spread * jax.random.normal(own_key, extent, jnp.float32)
    if split:
        values = values * level_of(own_key, extent, split, -0.22, 0.18)
    return jnp.clip(raised(values, jax.random.fold_in(own_key, 3), *heavy), -reach, reach).astype(held_as)


def setup_inputs(seed: int = 0) -> dict:
    key_of = jax.random.split(jax.random.key(seed), 12)
    tokens = normal_values(key_of[0], (TOKENS, D), 1.0, 6.0, ((0, 32), (1, 16)))
    expert_ids_keys = jax.random.split(jax.random.fold_in(key_of[1], 1), TOKENS // TOK_DEV)
    expert_ids_turns = jax.random.permutation(jax.random.fold_in(key_of[1], 3), TOKENS // TOK_DEV)
    expert_ids = jax.vmap(lambda own, number: assign_block(jax.random.fold_in(key_of[1], 2), own, number, TOK_DEV, EXPERTS, TOP, CAP, 2))(expert_ids_keys, expert_ids_turns).reshape((TOKENS, TOP))
    route_weights = jnp.clip(jnp.exp(math.log(0.6) - 2.4849067 * jax.random.uniform(key_of[2], (TOKENS, TOP), jnp.float32) ** level_of(key_of[2], (TOKENS, TOP), ((0, 32),), -0.2, 0.2)), 0.05, 0.6)
    routed_gate = normal_values(key_of[3], (EXPERTS, HID, D), D ** -0.5, 0.078125, ((0, 32), (1, 16)))
    routed_up = normal_values(key_of[4], (EXPERTS, HID, D), D ** -0.5, 0.078125, ((0, 32), (1, 16)))
    routed_down = normal_values(key_of[5], (EXPERTS, HID, D), HID ** -0.5, 0.15625, ((0, 32), (2, 16)))
    shared_gate = normal_values(key_of[6], (D, SH), D ** -0.5, 0.078125, ((0, 32), (1, 16)))
    shared_up = normal_values(key_of[7], (D, SH), D ** -0.5, 0.078125, ((0, 32), (1, 16)))
    shared_down = heavy_noise(key_of[8], (SH, D), SH ** -0.5, 0.21875, ((0, 16), (1, 32)), (0, 1, 32, 2.75))
    norm_gain = jnp.clip(1.0 + 0.15 * jax.random.normal(key_of[9], (D,), jnp.float32), 0.25, 1.75)
    proj_weight = normal_values(key_of[10], (QA + KVA, D), D ** -0.5, 0.078125, ((0, 16),))
    return dict(tokens=tokens, expert_ids=expert_ids, route_weights=route_weights, routed_gate=routed_gate, routed_up=routed_up, routed_down=routed_down, shared_gate=shared_gate, shared_up=shared_up, shared_down=shared_down, norm_gain=norm_gain, proj_weight=proj_weight)


def swiglu(gate, up):
    return (jax.nn.silu(gate) * up).astype(jnp.bfloat16)

def reference(tokens, expert_ids, route_weights, routed_gate, routed_up, routed_down, shared_gate, shared_up, shared_down, norm_gain, proj_weight):
    blocks = TOKENS // TOK_DEV
    flat_ids = expert_ids.reshape(blocks, TOK_DEV * TOP)
    onehot = (flat_ids[:, :, None] == jnp.arange(EXPERTS, dtype=jnp.int32)[None, None, :]).astype(jnp.int32)
    slots = lax.optimization_barrier(jnp.sum((jnp.cumsum(onehot, axis=1) - onehot) * onehot, axis=2)).astype(jnp.int32)
    block_of = jnp.repeat(jnp.arange(blocks, dtype=jnp.int32), TOK_DEV * TOP).reshape(blocks, TOK_DEV * TOP)
    owners = jnp.repeat(jnp.arange(TOKENS, dtype=jnp.int32), TOP).reshape(blocks, TOK_DEV * TOP)
    place = (block_of * CAP + slots).astype(jnp.int32)
    sources = jnp.full((EXPERTS, blocks * CAP), TOKENS, jnp.int32).at[flat_ids, place].set(owners)
    weights = jnp.zeros((EXPERTS, blocks * CAP), jnp.float32).at[flat_ids, place].set(route_weights.reshape(blocks, TOK_DEV * TOP))
    padded = jnp.concatenate([tokens, jnp.zeros((1, D), tokens.dtype)], axis=0)

    def one_expert(carry, items):
        gate_w, up_w, down_w, src, wts = items
        rows = padded[src]
        hidden = swiglu(jnp.dot(rows, gate_w.T, preferred_element_type=jnp.float32), jnp.dot(rows, up_w.T, preferred_element_type=jnp.float32))
        out = jnp.dot(hidden, down_w, preferred_element_type=jnp.float32).astype(jnp.bfloat16)
        out = lax.optimization_barrier(out).astype(jnp.float32)
        return (carry.at[src].add(wts[:, None] * out), None)
    start = jnp.zeros((TOKENS + 1, D), jnp.float32)
    routed, _ = lax.scan(one_expert, start, (routed_gate, routed_up, routed_down, sources, weights))
    routed = routed[:TOKENS]
    shared_hidden = swiglu(jnp.dot(tokens, shared_gate, preferred_element_type=jnp.float32), jnp.dot(tokens, shared_up, preferred_element_type=jnp.float32))
    shared = jnp.dot(shared_hidden, shared_down, preferred_element_type=jnp.float32)
    stream = (tokens.astype(jnp.float32) + shared + routed).astype(jnp.bfloat16)
    values = stream.astype(jnp.float32)
    scale = lax.rsqrt(lax.optimization_barrier(jnp.mean(values * values, axis=1, keepdims=True)) + 1e-06)
    normed = (values * scale * norm_gain[None, :]).astype(jnp.bfloat16)
    projected = jnp.dot(normed, proj_weight.T, preferred_element_type=jnp.float32).astype(jnp.bfloat16)
    return (stream, projected)
```

```python
import jax
import jax.numpy as jnp
from jax import lax
from jax.sharding import PartitionSpec as P

ROWS = 16
CHIPS = 8
LANES = [[x * ROWS + z for z in range(ROWS)] for x in range(2)]
SIDES = [[2 * chip + core for chip in range(CHIPS)] for core in range(2)]


def dot(left, right, over_left, over_right):
    return lax.dot_general(
        left, right, (((over_left,), (over_right,)), ((), ())), preferred_element_type=jnp.float32
    )


def exchange(parts, axis, groups=None):
    return lax.all_to_all(
        parts, axis, split_axis=0, concat_axis=0, tiled=True, axis_index_groups=groups
    )


def gather_halves(block):
    mine = exchange(jnp.broadcast_to(block[None], (CHIPS,) + block.shape), "tensor", SIDES)
    theirs = lax.ppermute(mine, "tensor", [(i, i ^ 1) for i in range(2 * CHIPS)])
    return mine, theirs


def per_device(
    tokens,
    expert_ids,
    route_weights,
    routed_gate,
    routed_up,
    routed_down,
    shared_gate,
    shared_up,
    shared_down,
    norm_gain,
    proj_weight,
):
    tok, width = tokens.shape
    top = expert_ids.shape[1]
    experts = lax.axis_size("expert")
    cap = min(tok, 2 * tok * top // experts)
    slots = experts * cap
    bf16, f32 = jnp.bfloat16, jnp.float32
    side = lax.axis_index("tensor") % 2
    column = lax.axis_index("expert") // ROWS

    own = jnp.concatenate([shared_gate, shared_up, shared_down.T], axis=1)
    other = lax.ppermute(own, "expert", [(i, (i + ROWS) % (2 * ROWS)) for i in range(2 * ROWS)])
    pair = jnp.where(column == 0, jnp.stack([own, other]), jnp.stack([other, own]))
    gathered = lax.all_gather(pair, "expert", axis=0, axis_index_groups=LANES)

    match = expert_ids[:, :, None] == jnp.arange(experts, dtype=jnp.int32)[None, None, :]
    named = jnp.any(match, axis=1)
    weight = jnp.sum(jnp.where(match, route_weights[:, :, None], 0.0), axis=1)
    earlier = jnp.tril(jnp.ones((tok, tok), f32), -1)
    slot = jnp.dot(earlier, named.astype(f32)).astype(jnp.int32)
    chosen = named[:, :, None] & (
        slot[:, :, None] == jnp.arange(cap, dtype=jnp.int32)[None, None, :]
    )
    chosen = chosen.reshape(tok, slots)
    outgoing = dot(chosen.astype(bf16), tokens, 0, 0).astype(bf16)
    arrived = exchange(outgoing.reshape(experts, cap, width), "expert")
    rows = jnp.concatenate([arrived.reshape(slots, width), tokens], axis=0)

    def by_side(array, axis):
        size = array.shape[axis] // (2 * CHIPS)
        pieces = [lax.slice_in_dim(array, k * size, (k + 1) * size, axis=axis) for k in range(2 * CHIPS)]
        even, odd = (jnp.concatenate(pieces[k::2], axis=axis) for k in range(2))
        return jnp.where(side == 0, even, odd), jnp.where(side == 0, odd, even)

    gate_up = jnp.concatenate([routed_gate[0], routed_up[0]], axis=0)
    hid = routed_gate.shape[1]
    in_mine, in_theirs = by_side(gate_up, 1)
    out_mine, out_theirs = by_side(routed_down[0], 0)

    mine, theirs = gather_halves(rows.T)
    total = slots + tok
    both = dot(in_mine, mine.reshape(-1, total), 1, 0) + dot(in_theirs, theirs.reshape(-1, total), 1, 0)
    hidden = (jax.nn.silu(both[:hid, :slots]) * both[hid:, :slots]).astype(bf16)
    hidden_mine, hidden_theirs = gather_halves(hidden)
    result = dot(hidden_mine.reshape(-1, slots), out_mine, 0, 0) + dot(
        hidden_theirs.reshape(-1, slots), out_theirs, 0, 0
    )
    returned = exchange(result.astype(bf16).reshape(experts, cap, width), "expert")
    scaled = jnp.where(chosen, jnp.repeat(weight, cap, axis=1), 0.0)
    high = lax.reduce_precision(scaled, 8, 7)
    split = jnp.concatenate([high, scaled - high], axis=0).astype(bf16)
    terms = dot(split, returned.reshape(slots, width), 1, 0)
    routed = terms[:tok] + terms[tok:]

    half_mine, half_theirs = mine[:, :, slots:], theirs[:, :, slots:]
    even = jnp.where(side == 0, half_mine, half_theirs)
    odd = jnp.where(side == 0, half_theirs, half_mine)
    features = jnp.stack([even, odd], axis=1).reshape(2, ROWS, -1, tok)
    features = jnp.swapaxes(features, 0, 1).reshape(-1, tok)
    table = gathered.reshape(-1, gathered.shape[-1])
    inner = shared_gate.shape[1]
    sums = dot(features, table[:, : 2 * inner], 0, 0)
    shared_hidden = (jax.nn.silu(sums[:, :inner]) * sums[:, inner:]).astype(bf16)
    partial = dot(shared_hidden, table[:, 2 * inner :], 1, 1).astype(bf16)
    partial = partial.reshape(tok, ROWS, 2, -1)
    partial = jnp.transpose(partial, (2, 1, 0, 3)).reshape(2 * CHIPS, 2, tok, -1)
    partial = jnp.concatenate([partial[:, 0], partial[:, 1]], axis=2)
    shared = jnp.sum(exchange(partial, "tensor").astype(f32), axis=0)

    stream = (tokens.astype(f32) + shared + routed).astype(bf16)
    spread = exchange(jnp.broadcast_to(stream[None], (2 * CHIPS,) + stream.shape), "tensor")
    values = jnp.swapaxes(spread, 0, 1).reshape(tok, -1).astype(f32)
    scale = lax.rsqrt(jnp.mean(values * values, axis=1, keepdims=True) + 1e-06)
    normed = (values * scale * norm_gain[None, :]).astype(bf16)
    projected = dot(normed, proj_weight, 1, 1).astype(bf16)
    return (stream, projected)


def solution(mesh):
    in_specs = (
        P("expert", "tensor"),
        P("expert", None),
        P("expert", None),
        P("expert", "tensor", None),
        P("expert", "tensor", None),
        P("expert", None, "tensor"),
        P("expert", "tensor"),
        P("expert", "tensor"),
        P("tensor", "expert"),
        P(),
        P("tensor", None),
    )
    out_specs = (P("expert", "tensor"), P("expert", "tensor"))
    return jax.shard_map(
        per_device, mesh=mesh, in_specs=in_specs, out_specs=out_specs, check_vma=False
    )
```

```python
import jax
import jax.numpy as jnp
import numpy as np
from jax import lax
from jax.sharding import PartitionSpec as P

ROWS = 16
PACK = 48
CHIPS = 8
LANES = [[x * ROWS + z for z in range(ROWS)] for x in range(2)]
SIDES = [[2 * chip + core for chip in range(CHIPS)] for core in range(2)]


def dot(left, right, over_left, over_right):
    return lax.dot_general(
        left, right, (((over_left,), (over_right,)), ((), ())), preferred_element_type=jnp.float32
    )


def exchange(parts, axis, groups=None):
    return lax.all_to_all(
        parts, axis, split_axis=0, concat_axis=0, tiled=True, axis_index_groups=groups
    )


def gather_halves(block):
    mine = exchange(jnp.broadcast_to(block[None], (CHIPS,) + block.shape), "tensor", SIDES)
    theirs = lax.ppermute(mine, "tensor", [(i, i ^ 1) for i in range(2 * CHIPS)])
    return mine, theirs


def packed(rows):
    half = rows.shape[1] // 2
    tail = jnp.concatenate([rows[:, :half, 256:], rows[:, half:, 256:]], axis=2)
    flat = jnp.concatenate([rows[:, :, :128], rows[:, :, 128:256], tail], axis=1)
    return jnp.pad(flat, ((0, 0), (0, PACK - flat.shape[1]), (0, 0)))


def unpacked(flat, cap):
    tail = flat[:, 2 * cap : 2 * cap + cap // 2]
    tail = jnp.concatenate([tail[:, :, :64], tail[:, :, 64:]], axis=1)
    return jnp.concatenate([flat[:, :cap], flat[:, cap : 2 * cap], tail], axis=2)


def per_device(
    tokens,
    expert_ids,
    route_weights,
    routed_gate,
    routed_up,
    routed_down,
    shared_gate,
    shared_up,
    shared_down,
    norm_gain,
    proj_weight,
):
    tok, width = tokens.shape
    top = expert_ids.shape[1]
    experts = lax.axis_size("expert")
    cap = min(tok, 2 * tok * top // experts)
    slots = experts * cap
    bf16, f32 = jnp.bfloat16, jnp.float32
    rank = lax.axis_index("tensor")
    side, across, ring = rank & 1, (rank >> 1) & 1, rank >> 2
    column = lax.axis_index("expert") >> 4

    match = expert_ids[:, :, None] == jnp.arange(experts, dtype=jnp.int32)[None, None, :]
    named = jnp.any(match, axis=1)
    weight = jnp.sum(jnp.where(match, route_weights[:, :, None], 0.0), axis=1)
    earlier = jnp.tril(jnp.ones((tok, tok), bf16), -1)
    slot = jnp.where(named, jnp.dot(earlier, named.astype(bf16), preferred_element_type=f32), -2.0)
    place = np.arange(experts * PACK)
    row = place % PACK
    spread = jnp.asarray(place[None, :] // PACK == np.arange(experts)[:, None], bf16)
    tail = (row >= 2 * cap) & (row < 2 * cap + cap // 2)
    held = np.stack(
        [
            np.where(row < cap, row, -1),
            np.where((row >= cap) & (row < 2 * cap), row - cap, -1),
            np.where(tail, row - 2 * cap, -1),
            np.where(tail, row - 2 * cap + cap // 2, -1),
        ]
    )
    wide = jnp.dot(slot.astype(bf16), spread, preferred_element_type=f32).astype(bf16)
    chosen = wide[None] == jnp.asarray(held, bf16)[:, None, :]
    chosen = chosen.reshape(4 * tok, -1)
    blank = jnp.zeros((tok, 64), bf16)
    lanes = jnp.concatenate(
        [
            tokens[:, :128],
            tokens[:, 128:256],
            jnp.concatenate([tokens[:, 256:], blank], axis=1),
            jnp.concatenate([blank, tokens[:, 256:]], axis=1),
        ],
        axis=0,
    )
    outgoing = dot(chosen.astype(bf16), lanes, 0, 0).astype(bf16)
    arrived = exchange(outgoing.reshape(experts, PACK, 128), "expert")

    def by_side(array, axis):
        size = array.shape[axis] // (2 * CHIPS)
        pieces = [lax.slice_in_dim(array, k * size, (k + 1) * size, axis=axis) for k in range(2 * CHIPS)]
        even, odd = (jnp.concatenate(pieces[k::2], axis=axis) for k in range(2))
        return jnp.where(side == 0, even, odd), jnp.where(side == 0, odd, even)

    gate_up = jnp.concatenate([routed_gate[0], routed_up[0]], axis=0)
    hid = routed_gate.shape[1]
    in_mine, in_theirs = by_side(gate_up, 1)
    out_mine, out_theirs = by_side(routed_down[0], 0)

    own = jnp.concatenate([shared_gate, shared_up, shared_down.T], axis=1)
    other = lax.ppermute(own, "expert", [(i, (i + ROWS) % (2 * ROWS)) for i in range(2 * ROWS)])
    pair = jnp.where(column == 0, jnp.stack([own, other]), jnp.stack([other, own]))
    arrived, pair, in_mine, in_theirs, out_mine, out_theirs = lax.optimization_barrier(
        (arrived, pair, in_mine, in_theirs, out_mine, out_theirs)
    )
    gathered = lax.all_gather(pair, "expert", axis=0, axis_index_groups=LANES)

    rows = unpacked(arrived, cap).reshape(slots, width)
    rows = jnp.concatenate([rows, tokens], axis=0)
    mine, theirs = gather_halves(rows.T)
    total = slots + tok
    both = dot(in_mine, mine.reshape(-1, total), 1, 0) + dot(in_theirs, theirs.reshape(-1, total), 1, 0)
    hidden = (jax.nn.silu(both[:hid, :slots]) * both[hid:, :slots]).astype(bf16)
    hidden_mine, hidden_theirs = gather_halves(hidden)
    result = dot(hidden_mine.reshape(-1, slots), out_mine, 0, 0) + dot(
        hidden_theirs.reshape(-1, slots), out_theirs, 0, 0
    )
    returned = exchange(packed(result.astype(bf16).reshape(experts, cap, width)), "expert")
    half_mine, half_theirs = mine[:, :, slots:], theirs[:, :, slots:]
    even = jnp.where(side == 0, half_mine, half_theirs)
    odd = jnp.where(side == 0, half_theirs, half_mine)
    features = jnp.stack([even, odd], axis=1).reshape(2, ROWS, -1, tok)
    features = jnp.swapaxes(features, 0, 1).reshape(-1, tok)
    table = gathered.reshape(-1, gathered.shape[-1])
    inner = shared_gate.shape[1]
    sums = dot(features, table[:, : 2 * inner], 0, 0)
    shared_hidden = (jax.nn.silu(sums[:, :inner]) * sums[:, inner:]).astype(bf16)
    partial = dot(shared_hidden, table[:, 2 * inner :], 1, 1).astype(bf16)
    partial = partial.reshape(tok, ROWS, 2, -1)
    partial = jnp.transpose(partial, (2, 1, 0, 3)).reshape(2 * CHIPS, 2, tok, -1)
    partial = jnp.concatenate([partial[:, 0], partial[:, 1]], axis=2)

    def halve(blocks, mine_is_odd, flip):
        twos = blocks.reshape((-1, 2) + blocks.shape[1:])
        keep = jnp.where(mine_is_odd == 0, twos[:, 0], twos[:, 1])
        give = jnp.where(mine_is_odd == 0, twos[:, 1], twos[:, 0])
        got = lax.ppermute(give, "tensor", [(i, i ^ flip) for i in range(2 * CHIPS)])
        return keep.astype(f32) + got.astype(f32)

    partial = halve(partial, side, 1).astype(bf16)
    partial = halve(partial, across, 2)
    shared = lax.dynamic_index_in_dim(partial, ring, 0, keepdims=False)
    for step in range(1, 4):
        give = lax.dynamic_index_in_dim(partial.astype(bf16), (ring + step) & 3, 0, keepdims=False)
        got = lax.ppermute(
            give, "tensor", [(i, (i + 4 * step) % (2 * CHIPS)) for i in range(2 * CHIPS)]
        )
        shared = shared + got.astype(f32)

    returned, shared = lax.optimization_barrier((returned, shared))
    high = lax.reduce_precision(weight, 8, 7)
    parts = jnp.concatenate([high, weight - high], axis=0).astype(bf16)
    parts = jnp.dot(parts, spread, preferred_element_type=f32).astype(bf16).reshape(2, 1, tok, -1)
    scaled = jnp.where(chosen.reshape(1, 4, tok, -1), parts, jnp.zeros((), bf16))
    terms = dot(scaled.reshape(8 * tok, -1), returned.reshape(-1, 128), 1, 0)
    terms = terms.reshape(2, 4, tok, 128)
    terms = terms[0] + terms[1]
    routed = jnp.concatenate([terms[0], terms[1], terms[2, :, :64] + terms[3, :, 64:]], axis=1)

    stream = (tokens.astype(f32) + shared + routed).astype(bf16)
    copies = exchange(jnp.broadcast_to(stream[None], (2 * CHIPS,) + stream.shape), "tensor")
    values = jnp.swapaxes(copies, 0, 1).reshape(tok, -1).astype(f32)
    scale = lax.rsqrt(jnp.mean(values * values, axis=1, keepdims=True) + 1e-06)
    normed = (values * scale * norm_gain[None, :]).astype(bf16)
    projected = dot(normed, proj_weight, 1, 1).astype(bf16)
    return (stream, projected)


def solution(mesh):
    in_specs = (
        P("expert", "tensor"),
        P("expert", None),
        P("expert", None),
        P("expert", "tensor", None),
        P("expert", "tensor", None),
        P("expert", None, "tensor"),
        P("expert", "tensor"),
        P("expert", "tensor"),
        P("tensor", "expert"),
        P(),
        P("tensor", None),
    )
    out_specs = (P("expert", "tensor"), P("expert", "tensor"))
    return jax.shard_map(
        per_device, mesh=mesh, in_specs=in_specs, out_specs=out_specs, check_vma=False
    )
```

```python
import jax
import jax.numpy as jnp
import numpy as np
from jax import lax
from jax.experimental import pallas as pl
from jax.experimental.pallas import tpu as pltpu
from jax.sharding import PartitionSpec as P

ROWS = 16
CHIPS = 8
LANES = [[x * ROWS + z for z in range(ROWS)] for x in range(2)]
SIDES = [[2 * chip + core for chip in range(CHIPS)] for core in range(2)]


def dot(left, right, over_left, over_right):
    return lax.dot_general(
        left, right, (((over_left,), (over_right,)), ((), ())), preferred_element_type=jnp.float32
    )


def exchange(parts, axis, groups=None):
    return lax.all_to_all(
        parts, axis, split_axis=0, concat_axis=0, tiled=True, axis_index_groups=groups
    )


def gather_halves(block):
    mine = exchange(jnp.broadcast_to(block[None], (CHIPS,) + block.shape), "tensor", SIDES)
    theirs = lax.ppermute(mine, "tensor", [(i, i ^ 1) for i in range(2 * CHIPS)])
    return mine, theirs


def shared_kernel(side_ref, mine_ref, theirs_ref, table_ref, keep_ref, give_ref):
    side = side_ref[0]
    inner = table_ref.shape[3] // 3
    size = table_ref.shape[2]
    start = mine_ref.shape[2] // 2

    def weights(chip, half):
        first = 2 * (2 * (chip % 4) + half)
        return table_ref.at[pl.ds(first, 2), chip // 4]

    sums = jnp.zeros((mine_ref.shape[2], 2 * inner), jnp.float32)
    for chip in range(CHIPS):
        for ref, half in ((mine_ref, side), (theirs_ref, 1 - side)):
            block = weights(chip, half)[:, :, : 2 * inner].reshape(2 * size, 2 * inner)
            sums = sums + dot(ref[chip], block, 0, 0)
    sums = sums[start : start + keep_ref.shape[1]]
    gate, up = sums[:, :inner], sums[:, inner:]
    hidden = (gate * (1.0 / (1.0 + jnp.exp(-gate))) * up).astype(jnp.bfloat16)
    for chip in range(CHIPS):
        for ref, half in ((keep_ref, side), (give_ref, 1 - side)):
            block = weights(chip, half)[:, :, 2 * inner :].reshape(2 * size, inner)
            ref[chip] = dot(hidden, block, 1, 1).astype(ref.dtype)


def shared_partial(side, mine, theirs, table, tok):
    width = mine.shape[1]
    out = jax.ShapeDtypeStruct((CHIPS, tok, width), jnp.bfloat16)
    last = pl.BlockSpec((CHIPS, width, 128), lambda i: (0, 0, 4))
    whole = pl.BlockSpec(out.shape, lambda i: (0, 0, 0))
    return pl.pallas_call(
        shared_kernel,
        out_shape=(out, out),
        grid=(1,),
        in_specs=[
            pl.BlockSpec(memory_space=pltpu.SMEM),
            last,
            last,
            pl.BlockSpec(table.shape, lambda i: (0, 0, 0, 0), pipeline_mode=pl.Buffered(1)),
        ],
        out_specs=(whole, whole),
        compiler_params=pltpu.CompilerParams(vmem_limit_bytes=32 * 2**20),
        cost_estimate=pl.CostEstimate(flops=1000, bytes_accessed=1000, transcendentals=0),
    )(side.reshape(1), mine, theirs, table)


def per_device(
    tokens,
    expert_ids,
    route_weights,
    routed_gate,
    routed_up,
    routed_down,
    shared_gate,
    shared_up,
    shared_down,
    norm_gain,
    proj_weight,
):
    tok, width = tokens.shape
    top = expert_ids.shape[1]
    experts = lax.axis_size("expert")
    cap = min(tok, 2 * tok * top // experts)
    slots = experts * cap
    bf16, f32 = jnp.bfloat16, jnp.float32
    rank = lax.axis_index("tensor")
    side, across, ring = rank & 1, (rank >> 1) & 1, rank >> 2
    column = lax.axis_index("expert") >> 4

    match = expert_ids[:, :, None] == jnp.arange(experts, dtype=jnp.int32)[None, None, :]
    named = jnp.any(match, axis=1)
    weight = jnp.sum(jnp.where(match, route_weights[:, :, None], 0.0), axis=1)
    earlier = jnp.tril(jnp.ones((tok, tok), bf16), -1)
    slot = jnp.where(named, jnp.dot(earlier, named.astype(bf16), preferred_element_type=f32), -2.0)
    place = np.arange(slots)
    spread = jnp.asarray(place[None, :] // cap == np.arange(experts)[:, None], bf16)
    wide = jnp.dot(slot.astype(bf16), spread, preferred_element_type=f32)
    chosen = wide == jnp.asarray(place % cap, f32)[None, :]
    outgoing = dot(chosen.astype(bf16), tokens, 0, 0).astype(bf16)
    arrived = exchange(outgoing.reshape(experts, cap, width), "expert")

    def by_side(array, axis):
        size = array.shape[axis] // (2 * CHIPS)
        pieces = [lax.slice_in_dim(array, k * size, (k + 1) * size, axis=axis) for k in range(2 * CHIPS)]
        even, odd = (jnp.concatenate(pieces[k::2], axis=axis) for k in range(2))
        return jnp.where(side == 0, even, odd), jnp.where(side == 0, odd, even)

    gate_up = jnp.concatenate([routed_gate[0], routed_up[0]], axis=0)
    hid = routed_gate.shape[1]
    in_mine, in_theirs = by_side(gate_up, 1)
    out_mine, out_theirs = by_side(routed_down[0], 0)

    own = jnp.concatenate([shared_gate, shared_up, shared_down.T], axis=1)
    other = lax.ppermute(own, "expert", [(i, (i + ROWS) % (2 * ROWS)) for i in range(2 * ROWS)])
    pair = jnp.where(column == 0, jnp.stack([own, other]), jnp.stack([other, own]))
    arrived, pair, in_mine, in_theirs, out_mine, out_theirs = lax.optimization_barrier(
        (arrived, pair, in_mine, in_theirs, out_mine, out_theirs)
    )
    gathered = lax.all_gather(pair, "expert", axis=0, axis_index_groups=LANES)

    rows = jnp.concatenate([arrived.reshape(slots, width), tokens], axis=0)
    mine, theirs = gather_halves(rows.T)
    total = slots + tok
    both = dot(in_mine, mine.reshape(-1, total), 1, 0) + dot(in_theirs, theirs.reshape(-1, total), 1, 0)
    hidden = (jax.nn.silu(both[:hid, :slots]) * both[hid:, :slots]).astype(bf16)
    hidden_mine, hidden_theirs = gather_halves(hidden)
    result = dot(hidden_mine.reshape(-1, slots), out_mine, 0, 0) + dot(
        hidden_theirs.reshape(-1, slots), out_theirs, 0, 0
    )
    returned = exchange(result.astype(bf16).reshape(experts, cap, width), "expert")
    keep, give = shared_partial(side, mine, theirs, gathered, tok)

    got = lax.ppermute(give, "tensor", [(i, i ^ 1) for i in range(2 * CHIPS)])
    partial = (keep.astype(f32) + got.astype(f32)).astype(bf16)
    partial = partial.reshape((-1, 2) + partial.shape[1:])
    keep = jnp.where(across == 0, partial[:, 0], partial[:, 1])
    give = jnp.where(across == 0, partial[:, 1], partial[:, 0])
    got = lax.ppermute(give, "tensor", [(i, i ^ 2) for i in range(2 * CHIPS)])
    partial = keep.astype(f32) + got.astype(f32)
    shared = lax.dynamic_index_in_dim(partial, ring, 0, keepdims=False)
    for step in range(1, 4):
        give = lax.dynamic_index_in_dim(partial.astype(bf16), (ring + step) & 3, 0, keepdims=False)
        got = lax.ppermute(
            give, "tensor", [(i, (i + 4 * step) % (2 * CHIPS)) for i in range(2 * CHIPS)]
        )
        shared = shared + got.astype(f32)

    returned, shared = lax.optimization_barrier((returned, shared))
    high = lax.reduce_precision(weight, 8, 7)
    parts = jnp.concatenate([high, weight - high], axis=0).astype(bf16)
    parts = jnp.dot(parts, spread, preferred_element_type=f32).astype(bf16).reshape(2, tok, -1)
    scaled = jnp.where(chosen[None], parts, jnp.zeros((), bf16)).reshape(2 * tok, -1)
    terms = dot(scaled, returned.reshape(slots, width), 1, 0)
    routed = terms[:tok] + terms[tok:]

    stream = (tokens.astype(f32) + shared + routed).astype(bf16)
    copies = exchange(jnp.broadcast_to(stream[None], (2 * CHIPS,) + stream.shape), "tensor")
    values = jnp.swapaxes(copies, 0, 1).reshape(tok, -1).astype(f32)
    scale = lax.rsqrt(jnp.mean(values * values, axis=1, keepdims=True) + 1e-06)
    normed = (values * scale * norm_gain[None, :]).astype(bf16)
    projected = dot(normed, proj_weight, 1, 1).astype(bf16)
    return (stream, projected)


def solution(mesh):
    in_specs = (
        P("expert", "tensor"),
        P("expert", None),
        P("expert", None),
        P("expert", "tensor", None),
        P("expert", "tensor", None),
        P("expert", None, "tensor"),
        P("expert", "tensor"),
        P("expert", "tensor"),
        P("tensor", "expert"),
        P(),
        P("tensor", None),
    )
    out_specs = (P("expert", "tensor"), P("expert", "tensor"))
    return jax.shard_map(
        per_device, mesh=mesh, in_specs=in_specs, out_specs=out_specs, check_vma=False
    )
```

```python
import jax
import jax.numpy as jnp
import numpy as np
from jax import lax
from jax.experimental import pallas as pl
from jax.experimental.pallas import tpu as pltpu
from jax.sharding import PartitionSpec as P

ROWS = 16
CHIPS = 8
LANES = [[x * ROWS + z for z in range(ROWS)] for x in range(2)]
SIDES = [[2 * chip + core for chip in range(CHIPS)] for core in range(2)]


def dot(left, right, over_left, over_right):
    return lax.dot_general(
        left, right, (((over_left,), (over_right,)), ((), ())), preferred_element_type=jnp.float32
    )


def exchange(parts, axis, groups=None):
    return lax.all_to_all(
        parts, axis, split_axis=0, concat_axis=0, tiled=True, axis_index_groups=groups
    )


def gather_halves(block):
    mine = exchange(jnp.broadcast_to(block[None], (CHIPS,) + block.shape), "tensor", SIDES)
    theirs = lax.ppermute(mine, "tensor", [(i, i ^ 1) for i in range(2 * CHIPS)])
    return mine, theirs


def shared_kernel(rank_ref, mine_ref, theirs_ref, table_ref, keep_ref, give_ref):
    side, place = rank_ref[0] & 1, rank_ref[0] >> 1
    inner = table_ref.shape[3] // 3
    size = table_ref.shape[2]
    start = mine_ref.shape[2] // 2

    def weights(chip, half):
        first = 2 * (2 * (chip & 3) + half)
        return table_ref.at[pl.ds(first, 2), chip >> 2]

    sums = jnp.zeros((mine_ref.shape[2], 2 * inner), jnp.float32)
    for chip in range(CHIPS):
        for ref, half in ((mine_ref, side), (theirs_ref, 1 - side)):
            block = weights(chip, half)[:, :, : 2 * inner].reshape(2 * size, 2 * inner)
            sums = sums + dot(ref[chip], block, 0, 0)
    sums = sums[start : start + keep_ref.shape[1]]
    gate, up = sums[:, :inner], sums[:, inner:]
    hidden = (gate * (1.0 / (1.0 + jnp.exp(-gate))) * up).astype(jnp.bfloat16)
    for step in range(CHIPS):
        for ref, half in ((keep_ref, side), (give_ref, 1 - side)):
            block = weights(place ^ step, half)[:, :, 2 * inner :].reshape(2 * size, inner)
            ref[step] = dot(hidden, block, 1, 1).astype(ref.dtype)


def shared_partial(rank, mine, theirs, table, tok):
    width = mine.shape[1]
    out = jax.ShapeDtypeStruct((CHIPS, tok, width), jnp.bfloat16)
    last = pl.BlockSpec((CHIPS, width, 128), lambda i: (0, 0, 4))
    whole = pl.BlockSpec(out.shape, lambda i: (0, 0, 0))
    return pl.pallas_call(
        shared_kernel,
        out_shape=(out, out),
        grid=(1,),
        in_specs=[
            pl.BlockSpec(memory_space=pltpu.SMEM),
            last,
            last,
            pl.BlockSpec(table.shape, lambda i: (0, 0, 0, 0), pipeline_mode=pl.Buffered(1)),
        ],
        out_specs=(whole, whole),
        compiler_params=pltpu.CompilerParams(vmem_limit_bytes=32 * 2**20),
        cost_estimate=pl.CostEstimate(flops=1000, bytes_accessed=1000, transcendentals=0),
    )(rank.reshape(1), mine, theirs, table)


def per_device(
    tokens,
    expert_ids,
    route_weights,
    routed_gate,
    routed_up,
    routed_down,
    shared_gate,
    shared_up,
    shared_down,
    norm_gain,
    proj_weight,
):
    tok, width = tokens.shape
    top = expert_ids.shape[1]
    experts = lax.axis_size("expert")
    cap = min(tok, 2 * tok * top // experts)
    slots = experts * cap
    bf16, f32 = jnp.bfloat16, jnp.float32
    rank = lax.axis_index("tensor")
    side = rank & 1
    column = lax.axis_index("expert") >> 4

    match = expert_ids[:, :, None] == jnp.arange(experts, dtype=jnp.int32)[None, None, :]
    named = jnp.any(match, axis=1)
    weight = jnp.sum(jnp.where(match, route_weights[:, :, None], 0.0), axis=1)
    earlier = jnp.tril(jnp.ones((tok, tok), bf16), -1)
    slot = jnp.where(named, jnp.dot(earlier, named.astype(bf16), preferred_element_type=f32), -2.0)
    place = np.arange(slots)
    spread = jnp.asarray(place[None, :] // cap == np.arange(experts)[:, None], bf16)
    wide = jnp.dot(slot.astype(bf16), spread, preferred_element_type=f32)
    chosen = wide == jnp.asarray(place % cap, f32)[None, :]
    outgoing = dot(chosen.astype(bf16), tokens, 0, 0).astype(bf16)
    arrived = exchange(outgoing.reshape(experts, cap, width), "expert")

    def by_side(array, axis):
        size = array.shape[axis] // (2 * CHIPS)
        pieces = [lax.slice_in_dim(array, k * size, (k + 1) * size, axis=axis) for k in range(2 * CHIPS)]
        even, odd = (jnp.concatenate(pieces[k::2], axis=axis) for k in range(2))
        return jnp.where(side == 0, even, odd), jnp.where(side == 0, odd, even)

    gate_up = jnp.concatenate([routed_gate[0], routed_up[0]], axis=0)
    hid = routed_gate.shape[1]
    in_mine, in_theirs = by_side(gate_up, 1)
    out_mine, out_theirs = by_side(routed_down[0], 0)

    own = jnp.concatenate([shared_gate, shared_up, shared_down.T], axis=1)
    other = lax.ppermute(own, "expert", [(i, (i + ROWS) % (2 * ROWS)) for i in range(2 * ROWS)])
    first = arrived[0, 0, 0]
    column = column + jnp.where(first == first, 0, 2)
    pair = jnp.where(column == 0, jnp.stack([own, other]), jnp.stack([other, own]))
    pair, late, in_mine, in_theirs, out_mine, out_theirs = lax.optimization_barrier(
        (pair, tokens, in_mine, in_theirs, out_mine, out_theirs)
    )
    gathered = lax.all_gather(pair, "expert", axis=0, axis_index_groups=LANES)

    rows = jnp.concatenate([arrived.reshape(slots, width), late], axis=0)
    mine, theirs = gather_halves(rows.T)
    total = slots + tok
    both = dot(in_mine, mine.reshape(-1, total), 1, 0) + dot(in_theirs, theirs.reshape(-1, total), 1, 0)
    hidden = (jax.nn.silu(both[:hid, :slots]) * both[hid:, :slots]).astype(bf16)
    hidden_mine, hidden_theirs = gather_halves(hidden)
    result = dot(hidden_mine.reshape(-1, slots), out_mine, 0, 0) + dot(
        hidden_theirs.reshape(-1, slots), out_theirs, 0, 0
    )
    result = result.astype(bf16).reshape(experts, cap, width)
    returned = exchange(result, "expert")
    keep, give = shared_partial(rank, mine, theirs, gathered, tok)

    got = lax.ppermute(give, "tensor", [(i, i ^ 1) for i in range(2 * CHIPS)])
    partial = keep.astype(f32) + got.astype(f32)
    shared = partial[0]
    for step in range(1, CHIPS):
        give = partial[step].astype(bf16)
        got = lax.ppermute(give, "tensor", [(i, i ^ (2 * step)) for i in range(2 * CHIPS)])
        shared = shared + got.astype(f32)

    returned, shared = lax.optimization_barrier((returned, shared))
    high = lax.reduce_precision(weight, 8, 7)
    parts = jnp.concatenate([high, weight - high], axis=0).astype(bf16)
    parts = jnp.dot(parts, spread, preferred_element_type=f32).astype(bf16).reshape(2, tok, -1)
    scaled = jnp.where(chosen[None], parts, jnp.zeros((), bf16)).reshape(2 * tok, -1)
    terms = dot(scaled, returned.reshape(slots, width), 1, 0)
    routed = terms[:tok] + terms[tok:]

    stream = (tokens.astype(f32) + shared + routed).astype(bf16)
    copies = exchange(jnp.broadcast_to(stream[None], (2 * CHIPS,) + stream.shape), "tensor")
    values = jnp.swapaxes(copies, 0, 1).reshape(tok, -1).astype(f32)
    scale = lax.rsqrt(jnp.mean(values * values, axis=1, keepdims=True) + 1e-06)
    normed = (values * scale * norm_gain[None, :]).astype(bf16)
    projected = dot(normed, proj_weight, 1, 1).astype(bf16)
    return (stream, projected)


def solution(mesh):
    in_specs = (
        P("expert", "tensor"),
        P("expert", None),
        P("expert", None),
        P("expert", "tensor", None),
        P("expert", "tensor", None),
        P("expert", None, "tensor"),
        P("expert", "tensor"),
        P("expert", "tensor"),
        P("tensor", "expert"),
        P(),
        P("tensor", None),
    )
    out_specs = (P("expert", "tensor"), P("expert", "tensor"))
    return jax.shard_map(
        per_device, mesh=mesh, in_specs=in_specs, out_specs=out_specs, check_vma=False
    )
```

```python
import jax
import jax.numpy as jnp
import numpy as np
from jax import lax
from jax.experimental import pallas as pl
from jax.experimental.pallas import tpu as pltpu
from jax.sharding import PartitionSpec as P

ROWS = 16
CHIPS = 8
LANES = [[x * ROWS + z for z in range(ROWS)] for x in range(2)]
SIDES = [[2 * chip + core for chip in range(CHIPS)] for core in range(2)]


def dot(left, right, over_left, over_right):
    return lax.dot_general(
        left, right, (((over_left,), (over_right,)), ((), ())), preferred_element_type=jnp.float32
    )


def exchange(parts, axis, groups=None):
    return lax.all_to_all(
        parts, axis, split_axis=0, concat_axis=0, tiled=True, axis_index_groups=groups
    )


def gather_halves(block):
    mine = exchange(jnp.broadcast_to(block[None], (CHIPS,) + block.shape), "tensor", SIDES)
    theirs = lax.ppermute(mine, "tensor", [(i, i ^ 1) for i in range(2 * CHIPS)])
    return mine, theirs


def shared_kernel(rank_ref, mine_ref, theirs_ref, table_ref, keep_ref, give_ref):
    side, place = rank_ref[0] & 1, rank_ref[0] >> 1
    inner = table_ref.shape[3] // 3
    size = table_ref.shape[2]
    start = mine_ref.shape[2] // 2

    def weights(chip, half):
        first = 2 * (2 * (chip & 3) + half)
        return table_ref.at[pl.ds(first, 2), chip >> 2]

    sums = jnp.zeros((mine_ref.shape[2], 2 * inner), jnp.float32)
    for chip in range(CHIPS):
        for ref, half in ((mine_ref, side), (theirs_ref, 1 - side)):
            block = weights(chip, half)[:, :, : 2 * inner].reshape(2 * size, 2 * inner)
            sums = sums + dot(ref[chip], block, 0, 0)
    sums = sums[start : start + keep_ref.shape[1]]
    gate, up = sums[:, :inner], sums[:, inner:]
    hidden = (gate * (1.0 / (1.0 + jnp.exp(-gate))) * up).astype(jnp.bfloat16)
    for step in range(CHIPS):
        for ref, half in ((keep_ref, side), (give_ref, 1 - side)):
            block = weights(place ^ step, half)[:, :, 2 * inner :].reshape(2 * size, inner)
            ref[step] = dot(hidden, block, 1, 1).astype(ref.dtype)


def shared_partial(rank, mine, theirs, table, tok):
    width = mine.shape[1]
    out = jax.ShapeDtypeStruct((CHIPS, tok, width), jnp.bfloat16)
    last = pl.BlockSpec((CHIPS, width, 128), lambda i: (0, 0, 4))
    whole = pl.BlockSpec(out.shape, lambda i: (0, 0, 0))
    return pl.pallas_call(
        shared_kernel,
        out_shape=(out, out),
        grid=(1,),
        in_specs=[
            pl.BlockSpec(memory_space=pltpu.SMEM),
            last,
            last,
            pl.BlockSpec(table.shape, lambda i: (0, 0, 0, 0), pipeline_mode=pl.Buffered(1)),
        ],
        out_specs=(whole, whole),
        compiler_params=pltpu.CompilerParams(vmem_limit_bytes=56 * 2**20),
        cost_estimate=pl.CostEstimate(flops=1000, bytes_accessed=1000, transcendentals=0),
    )(rank.reshape(1), mine, theirs, table)


def per_device(
    tokens,
    expert_ids,
    route_weights,
    routed_gate,
    routed_up,
    routed_down,
    shared_gate,
    shared_up,
    shared_down,
    norm_gain,
    proj_weight,
):
    tok, width = tokens.shape
    top = expert_ids.shape[1]
    experts = lax.axis_size("expert")
    cap = min(tok, 2 * tok * top // experts)
    slots = experts * cap
    bf16, f32 = jnp.bfloat16, jnp.float32
    rank = lax.axis_index("tensor")
    side = rank & 1
    column = lax.axis_index("expert") >> 4

    match = expert_ids[:, :, None] == jnp.arange(experts, dtype=jnp.int32)[None, None, :]
    named = jnp.any(match, axis=1)
    weight = jnp.sum(jnp.where(match, route_weights[:, :, None], 0.0), axis=1)
    earlier = jnp.tril(jnp.ones((tok, tok), bf16), -1)
    slot = jnp.where(named, jnp.dot(earlier, named.astype(bf16), preferred_element_type=f32), -2.0)
    place = np.arange(slots)
    spread = jnp.asarray(place[None, :] // cap == np.arange(experts)[:, None], bf16)
    wide = jnp.dot(slot.astype(bf16), spread, preferred_element_type=f32)
    chosen = wide == jnp.asarray(place % cap, f32)[None, :]
    outgoing = dot(chosen.astype(bf16), tokens, 0, 0).astype(bf16)
    arrived = exchange(outgoing.reshape(experts, cap, width), "expert")

    def by_side(array, axis):
        size = array.shape[axis] // (2 * CHIPS)
        pieces = [lax.slice_in_dim(array, k * size, (k + 1) * size, axis=axis) for k in range(2 * CHIPS)]
        even, odd = (jnp.concatenate(pieces[k::2], axis=axis) for k in range(2))
        return jnp.where(side == 0, even, odd), jnp.where(side == 0, odd, even)

    hid = routed_gate.shape[1]
    gate_up = jnp.concatenate([routed_gate[0], routed_up[0]], axis=0)
    in_mine, in_theirs = by_side(gate_up, 1)
    out_mine, out_theirs = by_side(routed_down[0], 0)

    own = jnp.concatenate([shared_gate, shared_up, shared_down.T], axis=1)
    other = lax.ppermute(own, "expert", [(i, (i + ROWS) % (2 * ROWS)) for i in range(2 * ROWS)])
    first = outgoing[0, 0]
    column = column + jnp.where(first == first, 0, 2)
    pair = jnp.where(column == 0, jnp.stack([own, other]), jnp.stack([other, own]))
    late, in_mine, in_theirs, out_mine, out_theirs = lax.optimization_barrier(
        (tokens, in_mine, in_theirs, out_mine, out_theirs)
    )
    gathered = lax.all_gather(pair, "expert", axis=0, axis_index_groups=LANES)

    rows = jnp.concatenate([arrived.reshape(slots, width), late], axis=0)
    mine, theirs = gather_halves(rows.T)
    total = slots + tok
    both = dot(in_mine, mine.reshape(-1, total), 1, 0) + dot(in_theirs, theirs.reshape(-1, total), 1, 0)
    hidden = (jax.nn.silu(both[:hid, :slots]) * both[hid:, :slots]).astype(bf16)
    hidden_mine, hidden_theirs = gather_halves(hidden)
    result = dot(hidden_mine.reshape(-1, slots), out_mine, 0, 0) + dot(
        hidden_theirs.reshape(-1, slots), out_theirs, 0, 0
    )
    result = result.astype(bf16).reshape(experts, cap, width)
    returned = exchange(result, "expert")
    keep, give = shared_partial(rank, mine, theirs, gathered, tok)

    got = lax.ppermute(give, "tensor", [(i, i ^ 1) for i in range(2 * CHIPS)])
    partial = keep.astype(f32) + got.astype(f32)
    shared = partial[0]
    for step in range(1, CHIPS):
        give = partial[step].astype(bf16)
        got = lax.ppermute(give, "tensor", [(i, i ^ (2 * step)) for i in range(2 * CHIPS)])
        shared = shared + got.astype(f32)

    returned, shared = lax.optimization_barrier((returned, shared))
    high = lax.reduce_precision(weight, 8, 7)
    parts = jnp.concatenate([high, weight - high], axis=0).astype(bf16)
    parts = jnp.dot(parts, spread, preferred_element_type=f32).astype(bf16).reshape(2, tok, -1)
    scaled = jnp.where(chosen[None], parts, jnp.zeros((), bf16)).reshape(2 * tok, -1)
    terms = dot(scaled, returned.reshape(slots, width), 1, 0)
    routed = terms[:tok] + terms[tok:]

    stream = (tokens.astype(f32) + shared + routed).astype(bf16)
    copies = exchange(jnp.broadcast_to(stream[None], (2 * CHIPS,) + stream.shape), "tensor")
    values = jnp.swapaxes(copies, 0, 1).reshape(tok, -1).astype(f32)
    scale = lax.rsqrt(jnp.mean(values * values, axis=1, keepdims=True) + 1e-06)
    normed = (values * scale * norm_gain[None, :]).astype(bf16)
    projected = dot(normed, proj_weight, 1, 1).astype(bf16)
    return (stream, projected)


def solution(mesh):
    in_specs = (
        P("expert", "tensor"),
        P("expert", None),
        P("expert", None),
        P("expert", "tensor", None),
        P("expert", "tensor", None),
        P("expert", None, "tensor"),
        P("expert", "tensor"),
        P("expert", "tensor"),
        P("tensor", "expert"),
        P(),
        P("tensor", None),
    )
    out_specs = (P("expert", "tensor"), P("expert", "tensor"))
    return jax.shard_map(
        per_device, mesh=mesh, in_specs=in_specs, out_specs=out_specs, check_vma=False
    )
```

```python
import jax
import jax.numpy as jnp
import numpy as np
from jax import lax
from jax.experimental import pallas as pl
from jax.experimental.pallas import tpu as pltpu
from jax.sharding import PartitionSpec as P

ROWS = 16
CHIPS = 8
LANES = [[x * ROWS + z for z in range(ROWS)] for x in range(2)]
SIDES = [[2 * chip + core for chip in range(CHIPS)] for core in range(2)]


def dot(left, right, over_left, over_right):
    return lax.dot_general(
        left, right, (((over_left,), (over_right,)), ((), ())), preferred_element_type=jnp.float32
    )


def exchange(parts, axis, groups=None):
    return lax.all_to_all(
        parts, axis, split_axis=0, concat_axis=0, tiled=True, axis_index_groups=groups
    )


def gather_halves(block):
    mine = exchange(jnp.broadcast_to(block[None], (CHIPS,) + block.shape), "tensor", SIDES)
    theirs = lax.ppermute(mine, "tensor", [(i, i ^ 1) for i in range(2 * CHIPS)])
    return mine, theirs


def shared_kernel(rank_ref, mine_ref, theirs_ref, table_ref, out_ref):
    rank = rank_ref[0]
    inner = table_ref.shape[3] // 3
    size = table_ref.shape[2]
    start = mine_ref.shape[2] // 2

    def weights(device):
        return table_ref.at[pl.ds(2 * (device & 7), 2), device >> 3]

    sums = jnp.zeros((mine_ref.shape[2], 2 * inner), jnp.float32)
    for chip in range(CHIPS):
        for ref, core in ((mine_ref, rank & 1), (theirs_ref, 1 - (rank & 1))):
            block = weights(2 * chip + core)[:, :, : 2 * inner].reshape(2 * size, 2 * inner)
            sums = sums + dot(ref[chip], block, 0, 0)
    sums = sums[start : start + out_ref.shape[2]]
    gate, up = sums[:, :inner], sums[:, inner:]
    hidden = (gate * (1.0 / (1.0 + jnp.exp(-gate))) * up).astype(jnp.bfloat16)
    for near in range(4):
        for far in range(4):
            block = weights(rank ^ (near + 4 * far))[:, :, 2 * inner :].reshape(2 * size, inner)
            out_ref[near, far] = dot(hidden, block, 1, 1).astype(out_ref.dtype)


def shared_partial(rank, mine, theirs, table, tok):
    width = mine.shape[1]
    out = jax.ShapeDtypeStruct((4, 4, tok, width), jnp.bfloat16)
    last = pl.BlockSpec((CHIPS, width, 128), lambda i: (0, 0, 4))
    return pl.pallas_call(
        shared_kernel,
        out_shape=out,
        grid=(1,),
        in_specs=[
            pl.BlockSpec(memory_space=pltpu.SMEM),
            last,
            last,
            pl.BlockSpec(table.shape, lambda i: (0, 0, 0, 0), pipeline_mode=pl.Buffered(1)),
        ],
        out_specs=pl.BlockSpec(out.shape, lambda i: (0, 0, 0, 0)),
        compiler_params=pltpu.CompilerParams(vmem_limit_bytes=56 * 2**20),
        cost_estimate=pl.CostEstimate(flops=1000, bytes_accessed=1000, transcendentals=0),
    )(rank.reshape(1), mine, theirs, table)


def per_device(
    tokens,
    expert_ids,
    route_weights,
    routed_gate,
    routed_up,
    routed_down,
    shared_gate,
    shared_up,
    shared_down,
    norm_gain,
    proj_weight,
):
    tok, width = tokens.shape
    top = expert_ids.shape[1]
    experts = lax.axis_size("expert")
    cap = min(tok, 2 * tok * top // experts)
    slots = experts * cap
    bf16, f32 = jnp.bfloat16, jnp.float32
    rank = lax.axis_index("tensor")
    side = rank & 1
    column = lax.axis_index("expert") >> 4

    match = expert_ids[:, :, None] == jnp.arange(experts, dtype=jnp.int32)[None, None, :]
    named = jnp.any(match, axis=1)
    weight = jnp.sum(jnp.where(match, route_weights[:, :, None], 0.0), axis=1)
    earlier = jnp.tril(jnp.ones((tok, tok), bf16), -1)
    slot = jnp.where(named, jnp.dot(earlier, named.astype(bf16), preferred_element_type=f32), -2.0)
    place = np.arange(slots)
    spread = jnp.asarray(place[None, :] // cap == np.arange(experts)[:, None], bf16)
    wide = jnp.dot(slot.astype(bf16), spread, preferred_element_type=f32)
    chosen = wide == jnp.asarray(place % cap, f32)[None, :]
    outgoing = dot(chosen.astype(bf16), tokens, 0, 0).astype(bf16)
    arrived = exchange(outgoing.reshape(experts, cap, width), "expert")

    def by_side(array, axis):
        size = array.shape[axis] // (2 * CHIPS)
        pieces = [lax.slice_in_dim(array, k * size, (k + 1) * size, axis=axis) for k in range(2 * CHIPS)]
        even, odd = (jnp.concatenate(pieces[k::2], axis=axis) for k in range(2))
        return jnp.where(side == 0, even, odd), jnp.where(side == 0, odd, even)

    hid = routed_gate.shape[1]
    gate_up = jnp.concatenate([routed_gate[0], routed_up[0]], axis=0)
    in_mine, in_theirs = by_side(gate_up, 1)
    out_mine, out_theirs = by_side(routed_down[0], 0)

    own = jnp.concatenate([shared_gate, shared_up, shared_down.T], axis=1)
    other = lax.ppermute(own, "expert", [(i, (i + ROWS) % (2 * ROWS)) for i in range(2 * ROWS)])
    pair = jnp.where(column == 0, jnp.stack([own, other]), jnp.stack([other, own]))
    arrived, pair, in_mine, in_theirs, out_mine, out_theirs = lax.optimization_barrier(
        (arrived, pair, in_mine, in_theirs, out_mine, out_theirs)
    )
    gathered = lax.all_gather(pair, "expert", axis=0, axis_index_groups=LANES)

    rows = jnp.concatenate([arrived.reshape(slots, width), tokens], axis=0)
    mine, theirs = gather_halves(rows.T)
    total = slots + tok
    both = dot(in_mine, mine.reshape(-1, total), 1, 0) + dot(in_theirs, theirs.reshape(-1, total), 1, 0)
    hidden = (jax.nn.silu(both[:hid, :slots]) * both[hid:, :slots]).astype(bf16)
    hidden_mine, hidden_theirs = gather_halves(hidden)
    result = dot(hidden_mine.reshape(-1, slots), out_mine, 0, 0) + dot(
        hidden_theirs.reshape(-1, slots), out_theirs, 0, 0
    )
    result = result.astype(bf16).reshape(experts, cap, width)
    returned = exchange(result, "expert")
    partial = shared_partial(rank, mine, theirs, gathered, tok)

    def summed(parts, stride):
        total = parts[0].astype(f32)
        for k in range(1, 4):
            perm = [(i, i ^ (k * stride)) for i in range(2 * CHIPS)]
            total = total + lax.ppermute(parts[k], "tensor", perm).astype(f32)
        return total

    shared = summed(summed(partial, 1).astype(bf16), 4)

    returned, shared = lax.optimization_barrier((returned, shared))
    high = lax.reduce_precision(weight, 8, 7)
    parts = jnp.concatenate([high, weight - high], axis=0).astype(bf16)
    parts = jnp.dot(parts, spread, preferred_element_type=f32).astype(bf16).reshape(2, tok, -1)
    scaled = jnp.where(chosen[None], parts, jnp.zeros((), bf16)).reshape(2 * tok, -1)
    terms = dot(scaled, returned.reshape(slots, width), 1, 0)
    routed = terms[:tok] + terms[tok:]

    stream = (tokens.astype(f32) + shared + routed).astype(bf16)
    copies = exchange(jnp.broadcast_to(stream[None], (2 * CHIPS,) + stream.shape), "tensor")
    values = jnp.swapaxes(copies, 0, 1).reshape(tok, -1).astype(f32)
    scale = lax.rsqrt(jnp.mean(values * values, axis=1, keepdims=True) + 1e-06)
    normed = (values * scale * norm_gain[None, :]).astype(bf16)
    projected = dot(normed, proj_weight, 1, 1).astype(bf16)
    return (stream, projected)


def solution(mesh):
    in_specs = (
        P("expert", "tensor"),
        P("expert", None),
        P("expert", None),
        P("expert", "tensor", None),
        P("expert", "tensor", None),
        P("expert", None, "tensor"),
        P("expert", "tensor"),
        P("expert", "tensor"),
        P("tensor", "expert"),
        P(),
        P("tensor", None),
    )
    out_specs = (P("expert", "tensor"), P("expert", "tensor"))
    return jax.shard_map(
        per_device, mesh=mesh, in_specs=in_specs, out_specs=out_specs, check_vma=False
    )
```

```python
import jax
import jax.numpy as jnp
import numpy as np
from jax import lax
from jax.experimental import pallas as pl
from jax.experimental.pallas import tpu as pltpu
from jax.sharding import PartitionSpec as P

ROWS = 16
CHIPS = 8
LANES = [[x * ROWS + z for z in range(ROWS)] for x in range(2)]
SIDES = [[2 * chip + core for chip in range(CHIPS)] for core in range(2)]
RINGS = [[4 * y + near for y in range(4)] for near in range(4)]


def dot(left, right, over_left, over_right):
    return lax.dot_general(
        left, right, (((over_left,), (over_right,)), ((), ())), preferred_element_type=jnp.float32
    )


def exchange(parts, axis, groups=None):
    return lax.all_to_all(
        parts, axis, split_axis=0, concat_axis=0, tiled=True, axis_index_groups=groups
    )


def gather_halves(block, groups, held=None):
    spread = jnp.broadcast_to(block[None], (len(groups[0]),) + block.shape)
    mine = exchange(spread, "tensor", groups)
    if held is not None:
        mine, held = lax.optimization_barrier((mine, held))
    theirs = lax.ppermute(mine, "tensor", [(i, i ^ 1) for i in range(2 * CHIPS)])
    return mine, theirs, held


def shared_kernel(rank_ref, mine_ref, far_mine_ref, theirs_ref, far_theirs_ref, table_ref, out_ref):
    rank = rank_ref[0]
    inner = table_ref.shape[3] // 3
    size = table_ref.shape[2]
    tok = out_ref.shape[2]

    def weights(device):
        return table_ref.at[pl.ds(2 * (device & 7), 2), device >> 3]

    def product(refs, across):
        total = jnp.zeros((mine_ref.shape[2], 2 * inner), jnp.float32)
        for y in range(4):
            for core in range(2):
                device = 4 * y + (((rank & 3) ^ (2 * across)) ^ core)
                block = weights(device)[:, :, : 2 * inner].reshape(2 * size, 2 * inner)
                total = total + dot(refs[core][y], block, 0, 0)
        return total

    sums = product((mine_ref, theirs_ref), 0)[64 : 64 + tok]
    sums = sums + product((far_mine_ref, far_theirs_ref), 1)[:tok]
    gate, up = sums[:, :inner], sums[:, inner:]
    hidden = (gate * (1.0 / (1.0 + jnp.exp(-gate))) * up).astype(jnp.bfloat16)
    for near in range(4):
        for far in range(4):
            block = weights(rank ^ (near + 4 * far))[:, :, 2 * inner :].reshape(2 * size, inner)
            out_ref[near, far] = dot(hidden, block, 1, 1).astype(out_ref.dtype)


def shared_partial(rank, mine, theirs, table, tok):
    width = mine.shape[1]
    out = jax.ShapeDtypeStruct((4, 4, tok, width), jnp.bfloat16)
    near = pl.BlockSpec((4, width, 128), lambda i: (0, 0, 4))
    far = pl.BlockSpec((4, width, 128), lambda i: (0, 0, 5))
    return pl.pallas_call(
        shared_kernel,
        out_shape=out,
        grid=(1,),
        in_specs=[
            pl.BlockSpec(memory_space=pltpu.SMEM),
            near,
            far,
            near,
            far,
            pl.BlockSpec(table.shape, lambda i: (0, 0, 0, 0), pipeline_mode=pl.Buffered(1)),
        ],
        out_specs=pl.BlockSpec(out.shape, lambda i: (0, 0, 0, 0)),
        compiler_params=pltpu.CompilerParams(vmem_limit_bytes=56 * 2**20),
        cost_estimate=pl.CostEstimate(flops=1000, bytes_accessed=1000, transcendentals=0),
    )(rank.reshape(1), mine, mine, theirs, theirs, table)


def per_device(
    tokens,
    expert_ids,
    route_weights,
    routed_gate,
    routed_up,
    routed_down,
    shared_gate,
    shared_up,
    shared_down,
    norm_gain,
    proj_weight,
):
    tok, width = tokens.shape
    top = expert_ids.shape[1]
    experts = lax.axis_size("expert")
    cap = min(tok, 2 * tok * top // experts)
    slots = experts * cap
    bf16, f32 = jnp.bfloat16, jnp.float32
    rank = lax.axis_index("tensor")
    side = rank & 1
    column = lax.axis_index("expert") >> 4

    match = expert_ids[:, :, None] == jnp.arange(experts, dtype=jnp.int32)[None, None, :]
    named = jnp.any(match, axis=1)
    weight = jnp.sum(jnp.where(match, route_weights[:, :, None], 0.0), axis=1)
    earlier = jnp.tril(jnp.ones((tok, tok), bf16), -1)
    slot = jnp.where(named, jnp.dot(earlier, named.astype(bf16), preferred_element_type=f32), -2.0)
    place = np.arange(slots)
    spread = jnp.asarray(place[None, :] // cap == np.arange(experts)[:, None], bf16)
    wide = jnp.dot(slot.astype(bf16), spread, preferred_element_type=f32)
    chosen = wide == jnp.asarray(place % cap, f32)[None, :]
    outgoing = dot(chosen.astype(bf16), tokens, 0, 0).astype(bf16)
    arrived = exchange(outgoing.reshape(experts, cap, width), "expert")

    def by_side(array, axis):
        size = array.shape[axis] // (2 * CHIPS)
        pieces = [lax.slice_in_dim(array, k * size, (k + 1) * size, axis=axis) for k in range(2 * CHIPS)]
        even, odd = (jnp.concatenate(pieces[k::2], axis=axis) for k in range(2))
        return jnp.where(side == 0, even, odd), jnp.where(side == 0, odd, even)

    hid = routed_gate.shape[1]
    gate_up = jnp.concatenate([routed_gate[0], routed_up[0]], axis=0)
    near = [jnp.concatenate([gate_up[:, k * width : (k + 1) * width] for k in range(low, 16, 4)], axis=1) for low in range(4)]

    def columns(flip):
        low = (rank & 3) ^ flip
        return jnp.where(low < 2, jnp.where(low == 0, near[0], near[1]), jnp.where(low == 2, near[2], near[3]))

    in_mine, in_theirs = columns(0), columns(1)
    give = jnp.concatenate([columns(2), columns(3)], axis=1)
    out_mine, out_theirs = by_side(routed_down[0], 0)

    own = jnp.concatenate([shared_gate, shared_up, shared_down.T], axis=1)
    other = lax.ppermute(own, "expert", [(i, (i + ROWS) % (2 * ROWS)) for i in range(2 * ROWS)])
    pair = jnp.where(column == 0, jnp.stack([own, other]), jnp.stack([other, own]))
    beside = lax.ppermute(tokens, "tensor", [(i, i ^ 2) for i in range(2 * CHIPS)])
    across = [(i, i ^ 2) for i in range(2 * CHIPS)]
    far_gate = lax.ppermute(give[:hid], "tensor", across)
    arrived, beside, pair, in_mine, in_theirs, give, far_gate, out_mine, out_theirs = lax.optimization_barrier(
        (arrived, beside, pair, in_mine, in_theirs, give, far_gate, out_mine, out_theirs)
    )
    far_up = lax.ppermute(give[hid:], "tensor", across)
    gathered = lax.all_gather(pair, "expert", axis=0, axis_index_groups=LANES)

    blank = jnp.zeros((16, width), bf16)
    rows = jnp.concatenate([arrived.reshape(slots, width), tokens, blank, beside], axis=0)
    mine, theirs, far_up = gather_halves(rows.T, RINGS, far_up)
    far = jnp.concatenate([far_gate, far_up], axis=0)
    total = rows.shape[0]
    left, right = mine.reshape(-1, total), theirs.reshape(-1, total)
    middle = left.shape[0]
    send = dot(far[:, :middle], left, 1, 0) + dot(far[:, middle:], right, 1, 0)
    got = lax.ppermute(send[:, :slots].astype(bf16), "tensor", [(i, i ^ 2) for i in range(2 * CHIPS)])
    both = dot(in_mine, left, 1, 0) + dot(in_theirs, right, 1, 0)
    both = both[:, :slots] + got.astype(f32)
    hidden = (jax.nn.silu(both[:hid]) * both[hid:]).astype(bf16)
    hidden_mine, hidden_theirs, _ = gather_halves(hidden, SIDES)
    result = dot(hidden_mine.reshape(-1, slots), out_mine, 0, 0) + dot(
        hidden_theirs.reshape(-1, slots), out_theirs, 0, 0
    )
    result = result.astype(bf16).reshape(experts, cap, width)
    returned = exchange(result, "expert")
    partial = shared_partial(rank, mine, theirs, gathered, tok)

    def summed(parts, stride):
        total = parts[0].astype(f32)
        for k in range(1, 4):
            perm = [(i, i ^ (k * stride)) for i in range(2 * CHIPS)]
            total = total + lax.ppermute(parts[k], "tensor", perm).astype(f32)
        return total

    shared = summed(summed(partial, 1).astype(bf16), 4)

    returned, shared = lax.optimization_barrier((returned, shared))
    high = lax.reduce_precision(weight, 8, 7)
    parts = jnp.concatenate([high, weight - high], axis=0).astype(bf16)
    parts = jnp.dot(parts, spread, preferred_element_type=f32).astype(bf16).reshape(2, tok, -1)
    scaled = jnp.where(chosen[None], parts, jnp.zeros((), bf16)).reshape(2 * tok, -1)
    terms = dot(scaled, returned.reshape(slots, width), 1, 0)
    routed = terms[:tok] + terms[tok:]

    stream = (tokens.astype(f32) + shared + routed).astype(bf16)
    copies = exchange(jnp.broadcast_to(stream[None], (2 * CHIPS,) + stream.shape), "tensor")
    values = jnp.swapaxes(copies, 0, 1).reshape(tok, -1).astype(f32)
    scale = lax.rsqrt(jnp.mean(values * values, axis=1, keepdims=True) + 1e-06)
    normed = (values * scale * norm_gain[None, :]).astype(bf16)
    projected = dot(normed, proj_weight, 1, 1).astype(bf16)
    return (stream, projected)


def solution(mesh):
    in_specs = (
        P("expert", "tensor"),
        P("expert", None),
        P("expert", None),
        P("expert", "tensor", None),
        P("expert", "tensor", None),
        P("expert", None, "tensor"),
        P("expert", "tensor"),
        P("expert", "tensor"),
        P("tensor", "expert"),
        P(),
        P("tensor", None),
    )
    out_specs = (P("expert", "tensor"), P("expert", "tensor"))
    return jax.shard_map(
        per_device, mesh=mesh, in_specs=in_specs, out_specs=out_specs, check_vma=False
    )
```

```python
import jax
import jax.numpy as jnp
import numpy as np
from jax import lax
from jax.experimental import pallas as pl
from jax.experimental.pallas import tpu as pltpu
from jax.sharding import PartitionSpec as P

ROWS = 16
CHIPS = 8
LANES = [[x * ROWS + z for z in range(ROWS)] for x in range(2)]
SIDES = [[2 * chip + core for chip in range(CHIPS)] for core in range(2)]
RINGS = [[4 * y + near for y in range(4)] for near in range(4)]


def dot(left, right, over_left, over_right):
    return lax.dot_general(
        left, right, (((over_left,), (over_right,)), ((), ())), preferred_element_type=jnp.float32
    )


def exchange(parts, axis, groups=None):
    return lax.all_to_all(
        parts, axis, split_axis=0, concat_axis=0, tiled=True, axis_index_groups=groups
    )


def gather_halves(block, groups, held=None):
    spread = jnp.broadcast_to(block[None], (len(groups[0]),) + block.shape)
    mine = exchange(spread, "tensor", groups)
    if held is not None:
        mine, held = lax.optimization_barrier((mine, held))
    theirs = lax.ppermute(mine, "tensor", [(i, i ^ 1) for i in range(2 * CHIPS)])
    return mine, theirs, held


def shared_kernel(rank_ref, mine_ref, far_mine_ref, theirs_ref, far_theirs_ref, table_ref, out_ref):
    rank = rank_ref[0]
    inner = table_ref.shape[3] // 3
    size = table_ref.shape[2]
    tok = out_ref.shape[2]

    def weights(device):
        return table_ref.at[pl.ds(2 * (device & 7), 2), device >> 3]

    def product(refs, across):
        total = jnp.zeros((mine_ref.shape[2], 2 * inner), jnp.float32)
        for y in range(4):
            for core in range(2):
                device = 4 * y + (((rank & 3) ^ (2 * across)) ^ core)
                block = weights(device)[:, :, : 2 * inner].reshape(2 * size, 2 * inner)
                total = total + dot(refs[core][y], block, 0, 0)
        return total

    sums = product((mine_ref, theirs_ref), 0)[64 : 64 + tok]
    sums = sums + product((far_mine_ref, far_theirs_ref), 1)[:tok]
    gate, up = sums[:, :inner], sums[:, inner:]
    hidden = (gate * (1.0 / (1.0 + jnp.exp(-gate))) * up).astype(jnp.bfloat16)
    for near in range(4):
        for far in range(4):
            block = weights(rank ^ (near + 4 * far))[:, :, 2 * inner :].reshape(2 * size, inner)
            out_ref[near, far] = dot(hidden, block, 1, 1).astype(out_ref.dtype)


def shared_partial(rank, mine, theirs, table, tok):
    width = mine.shape[1]
    out = jax.ShapeDtypeStruct((4, 4, tok, width), jnp.bfloat16)
    near = pl.BlockSpec((4, width, 128), lambda i: (0, 0, 4))
    far = pl.BlockSpec((4, width, 128), lambda i: (0, 0, 5))
    return pl.pallas_call(
        shared_kernel,
        out_shape=out,
        grid=(1,),
        in_specs=[
            pl.BlockSpec(memory_space=pltpu.SMEM),
            near,
            far,
            near,
            far,
            pl.BlockSpec(table.shape, lambda i: (0, 0, 0, 0), pipeline_mode=pl.Buffered(1)),
        ],
        out_specs=pl.BlockSpec(out.shape, lambda i: (0, 0, 0, 0)),
        compiler_params=pltpu.CompilerParams(vmem_limit_bytes=56 * 2**20),
        cost_estimate=pl.CostEstimate(flops=1000, bytes_accessed=1000, transcendentals=0),
    )(rank.reshape(1), mine, mine, theirs, theirs, table)


def norm_kernel(stream_ref, gain_ref, weight_ref, out_ref):
    blocks, _, width = stream_ref.shape
    squares = jnp.zeros(stream_ref.shape[1:], jnp.float32)
    for k in range(blocks):
        value = stream_ref[k].astype(jnp.float32)
        squares = squares + value * value
    mean = jnp.sum(squares, axis=1, keepdims=True) * (1.0 / (blocks * width))
    scale = lax.rsqrt(mean + 1e-06)
    total = jnp.zeros(out_ref.shape, jnp.float32)
    for k in range(0, blocks, 2):
        pair = [stream_ref[k + j].astype(jnp.float32) * scale for j in range(2)]
        pair = [(pair[j] * gain_ref[k + j : k + j + 1]).astype(jnp.bfloat16) for j in range(2)]
        total = total + dot(jnp.concatenate(pair, axis=1), weight_ref[:, k * width : (k + 2) * width], 1, 1)
    out_ref[...] = total.astype(out_ref.dtype)


def normed_product(copies, gain, weight):
    blocks, tok, width = copies.shape
    whole = pl.BlockSpec(memory_space=pltpu.VMEM)
    return pl.pallas_call(
        norm_kernel,
        out_shape=jax.ShapeDtypeStruct((tok, weight.shape[0]), jnp.bfloat16),
        in_specs=[whole, whole, whole],
        out_specs=whole,
        compiler_params=pltpu.CompilerParams(vmem_limit_bytes=24 * 2**20),
    )(copies, gain.reshape(blocks, width), weight)


def per_device(
    tokens,
    expert_ids,
    route_weights,
    routed_gate,
    routed_up,
    routed_down,
    shared_gate,
    shared_up,
    shared_down,
    norm_gain,
    proj_weight,
):
    tok, width = tokens.shape
    top = expert_ids.shape[1]
    experts = lax.axis_size("expert")
    cap = min(tok, 2 * tok * top // experts)
    slots = experts * cap
    bf16, f32 = jnp.bfloat16, jnp.float32
    rank = lax.axis_index("tensor")
    side = rank & 1
    column = lax.axis_index("expert") >> 4

    match = expert_ids[:, :, None] == jnp.arange(experts, dtype=jnp.int32)[None, None, :]
    named = jnp.any(match, axis=1)
    weight = jnp.sum(jnp.where(match, route_weights[:, :, None], 0.0), axis=1)
    earlier = jnp.tril(jnp.ones((tok, tok), bf16), -1)
    slot = jnp.where(named, jnp.dot(earlier, named.astype(bf16), preferred_element_type=f32), -2.0)
    place = np.arange(slots)
    spread = jnp.asarray(place[None, :] // cap == np.arange(experts)[:, None], bf16)
    wide = jnp.dot(slot.astype(bf16), spread, preferred_element_type=f32)
    chosen = wide == jnp.asarray(place % cap, f32)[None, :]
    outgoing = dot(chosen.astype(bf16), tokens, 0, 0).astype(bf16)
    arrived = exchange(outgoing.reshape(experts, cap, width), "expert")

    def by_side(array, axis):
        size = array.shape[axis] // (2 * CHIPS)
        pieces = [lax.slice_in_dim(array, k * size, (k + 1) * size, axis=axis) for k in range(2 * CHIPS)]
        even, odd = (jnp.concatenate(pieces[k::2], axis=axis) for k in range(2))
        return jnp.where(side == 0, even, odd), jnp.where(side == 0, odd, even)

    hid = routed_gate.shape[1]
    gate_up = jnp.concatenate([routed_gate[0], routed_up[0]], axis=0)
    near = [jnp.concatenate([gate_up[:, k * width : (k + 1) * width] for k in range(low, 16, 4)], axis=1) for low in range(4)]

    def columns(flip):
        low = (rank & 3) ^ flip
        return jnp.where(low < 2, jnp.where(low == 0, near[0], near[1]), jnp.where(low == 2, near[2], near[3]))

    in_mine, in_theirs = columns(0), columns(1)
    give = jnp.concatenate([columns(2), columns(3)], axis=1)
    out_mine, out_theirs = by_side(routed_down[0], 0)

    own = jnp.concatenate([shared_gate, shared_up, shared_down.T], axis=1)
    other = lax.ppermute(own, "expert", [(i, (i + ROWS) % (2 * ROWS)) for i in range(2 * ROWS)])
    pair = jnp.where(column == 0, jnp.stack([own, other]), jnp.stack([other, own]))
    across = [(i, i ^ 2) for i in range(2 * CHIPS)]
    give, late = lax.optimization_barrier((give, tokens))
    cut = give.shape[0] // 3
    far_first = lax.ppermute(give[:cut], "tensor", across)
    beside = lax.ppermute(late, "tensor", across)
    arrived, beside, pair, in_mine, in_theirs, give, far_first, out_mine, out_theirs = lax.optimization_barrier(
        (arrived, beside, pair, in_mine, in_theirs, give, far_first, out_mine, out_theirs)
    )
    far_rest = lax.ppermute(give[cut:], "tensor", across)
    gathered = lax.all_gather(pair, "expert", axis=0, axis_index_groups=LANES)

    blank = jnp.zeros((16, width), bf16)
    rows = jnp.concatenate([arrived.reshape(slots, width), tokens, blank, beside], axis=0)
    mine, theirs, far_rest = gather_halves(rows.T, RINGS, far_rest)
    far = jnp.concatenate([far_first, far_rest], axis=0)
    total = rows.shape[0]
    left, right = mine.reshape(-1, total), theirs.reshape(-1, total)
    middle = left.shape[0]
    send = dot(far[:, :middle], left, 1, 0) + dot(far[:, middle:], right, 1, 0)
    got = lax.ppermute(send[:, :slots].astype(bf16), "tensor", [(i, i ^ 2) for i in range(2 * CHIPS)])
    both = dot(in_mine, left, 1, 0) + dot(in_theirs, right, 1, 0)
    both = both[:, :slots] + got.astype(f32)
    hidden = (jax.nn.silu(both[:hid]) * both[hid:]).astype(bf16)
    hidden_mine, hidden_theirs, _ = gather_halves(hidden, SIDES)
    result = dot(hidden_mine.reshape(-1, slots), out_mine, 0, 0) + dot(
        hidden_theirs.reshape(-1, slots), out_theirs, 0, 0
    )
    result = result.astype(bf16).reshape(experts, cap, width)
    returned = exchange(result, "expert")
    partial = shared_partial(rank, mine, theirs, gathered, tok)

    def summed(parts, stride):
        total = parts[0].astype(f32)
        for k in range(1, 4):
            perm = [(i, i ^ (k * stride)) for i in range(2 * CHIPS)]
            total = total + lax.ppermute(parts[k], "tensor", perm).astype(f32)
        return total

    shared = summed(summed(partial, 1).astype(bf16), 4)

    returned, shared = lax.optimization_barrier((returned, shared))
    high = lax.reduce_precision(weight, 8, 7)
    parts = jnp.concatenate([high, weight - high], axis=0).astype(bf16)
    parts = jnp.dot(parts, spread, preferred_element_type=f32).astype(bf16).reshape(2, tok, -1)
    scaled = jnp.where(chosen[None], parts, jnp.zeros((), bf16)).reshape(2 * tok, -1)
    terms = dot(scaled, returned.reshape(slots, width), 1, 0)
    routed = terms[:tok] + terms[tok:]

    stream = (tokens.astype(f32) + shared + routed).astype(bf16)
    copies = exchange(jnp.broadcast_to(stream[None], (2 * CHIPS,) + stream.shape), "tensor")
    projected = normed_product(copies, norm_gain, proj_weight)
    return (stream, projected)


def solution(mesh):
    in_specs = (
        P("expert", "tensor"),
        P("expert", None),
        P("expert", None),
        P("expert", "tensor", None),
        P("expert", "tensor", None),
        P("expert", None, "tensor"),
        P("expert", "tensor"),
        P("expert", "tensor"),
        P("tensor", "expert"),
        P(),
        P("tensor", None),
    )
    out_specs = (P("expert", "tensor"), P("expert", "tensor"))
    return jax.shard_map(
        per_device, mesh=mesh, in_specs=in_specs, out_specs=out_specs, check_vma=False
    )
```

```python
import jax
import jax.numpy as jnp
import numpy as np
from jax import lax
from jax.experimental import pallas as pl
from jax.experimental.pallas import tpu as pltpu
from jax.sharding import PartitionSpec as P

ROWS = 16
CHIPS = 8
LANES = [[x * ROWS + z for z in range(ROWS)] for x in range(2)]
SIDES = [[2 * chip + core for chip in range(CHIPS)] for core in range(2)]
RINGS = [[4 * y + near for y in range(4)] for near in range(4)]


def dot(left, right, over_left, over_right):
    return lax.dot_general(
        left, right, (((over_left,), (over_right,)), ((), ())), preferred_element_type=jnp.float32
    )


def exchange(parts, axis, groups=None):
    return lax.all_to_all(
        parts, axis, split_axis=0, concat_axis=0, tiled=True, axis_index_groups=groups
    )


def gather_halves(block, groups, held=None):
    spread = jnp.broadcast_to(block[None], (len(groups[0]),) + block.shape)
    mine = exchange(spread, "tensor", groups)
    if held is not None:
        mine, held = lax.optimization_barrier((mine, held))
    theirs = lax.ppermute(mine, "tensor", [(i, i ^ 1) for i in range(2 * CHIPS)])
    return mine, theirs, held


def shared_kernel(rank_ref, mine_ref, far_mine_ref, theirs_ref, far_theirs_ref, table_ref, out_ref, hidden_ref):
    rank = rank_ref[0]
    inner = table_ref.shape[3] // 2
    size = table_ref.shape[2]
    tok = out_ref.shape[2]

    def weights(device):
        return table_ref.at[pl.ds(2 * (device & 7), 2), device >> 3]

    def product(refs, across):
        total = jnp.zeros((mine_ref.shape[2], 2 * inner), jnp.float32)
        for y in range(4):
            for core in range(2):
                device = 4 * y + (((rank & 3) ^ (2 * across)) ^ core)
                block = weights(device)[...].reshape(2 * size, 2 * inner)
                total = total + dot(refs[core][y], block, 0, 0)
        return total

    @pl.when(pl.program_id(0) == 0)
    def _():
        sums = product((mine_ref, theirs_ref), 0)[64 : 64 + tok]
        sums = sums + product((far_mine_ref, far_theirs_ref), 1)[:tok]
        gate, up = sums[:, :inner], sums[:, inner:]
        hidden_ref[...] = (gate * (1.0 / (1.0 + jnp.exp(-gate))) * up).astype(jnp.bfloat16)

    @pl.when(pl.program_id(0) == 1)
    def _():
        hidden = hidden_ref[...]
        for near in range(4):
            for far in range(4):
                block = weights(rank ^ (near + 4 * far))[:, :, :inner].reshape(2 * size, inner)
                out_ref[far, near] = dot(hidden, block, 1, 1).astype(out_ref.dtype)


def shared_partial(rank, mine, theirs, table, tok):
    width = mine.shape[1]
    columns = 2 * table.shape[3] // 3
    out = jax.ShapeDtypeStruct((4, 4, tok, width), jnp.bfloat16)
    near = pl.BlockSpec((4, width, 128), lambda i: (0, 0, 4))
    far = pl.BlockSpec((4, width, 128), lambda i: (0, 0, 5))
    return pl.pallas_call(
        shared_kernel,
        out_shape=out,
        grid=(2,),
        in_specs=[
            pl.BlockSpec(memory_space=pltpu.SMEM),
            near,
            far,
            near,
            far,
            pl.BlockSpec(table.shape[:3] + (columns,), lambda i: (0, 0, 0, i)),
        ],
        out_specs=pl.BlockSpec(out.shape, lambda i: (0, 0, 0, 0)),
        scratch_shapes=[pltpu.VMEM((tok, columns // 2), jnp.bfloat16)],
        compiler_params=pltpu.CompilerParams(vmem_limit_bytes=56 * 2**20),
        cost_estimate=pl.CostEstimate(flops=1000, bytes_accessed=1000, transcendentals=0),
    )(rank.reshape(1), mine, mine, theirs, theirs, table)


def norm_kernel(stream_ref, gain_ref, weight_ref, out_ref):
    blocks, _, width = stream_ref.shape
    squares = jnp.zeros(stream_ref.shape[1:], jnp.float32)
    for k in range(blocks):
        value = stream_ref[k].astype(jnp.float32)
        squares = squares + value * value
    mean = jnp.sum(squares, axis=1, keepdims=True) * (1.0 / (blocks * width))
    scale = lax.rsqrt(mean + 1e-06)
    total = jnp.zeros(out_ref.shape, jnp.float32)
    for k in range(0, blocks, 2):
        pair = [stream_ref[k + j].astype(jnp.float32) * scale for j in range(2)]
        pair = [(pair[j] * gain_ref[k + j : k + j + 1]).astype(jnp.bfloat16) for j in range(2)]
        total = total + dot(jnp.concatenate(pair, axis=1), weight_ref[:, k * width : (k + 2) * width], 1, 1)
    out_ref[...] = total.astype(out_ref.dtype)


def normed_product(copies, gain, weight):
    blocks, tok, width = copies.shape
    whole = pl.BlockSpec(memory_space=pltpu.VMEM)
    return pl.pallas_call(
        norm_kernel,
        out_shape=jax.ShapeDtypeStruct((tok, weight.shape[0]), jnp.bfloat16),
        in_specs=[whole, whole, whole],
        out_specs=whole,
        compiler_params=pltpu.CompilerParams(vmem_limit_bytes=24 * 2**20),
    )(copies, gain.reshape(blocks, width), weight)


def per_device(
    tokens,
    expert_ids,
    route_weights,
    routed_gate,
    routed_up,
    routed_down,
    shared_gate,
    shared_up,
    shared_down,
    norm_gain,
    proj_weight,
):
    tok, width = tokens.shape
    top = expert_ids.shape[1]
    experts = lax.axis_size("expert")
    cap = min(tok, 2 * tok * top // experts)
    slots = experts * cap
    bf16, f32 = jnp.bfloat16, jnp.float32
    rank = lax.axis_index("tensor")
    side = rank & 1
    column = lax.axis_index("expert") >> 4

    match = expert_ids[:, :, None] == jnp.arange(experts, dtype=jnp.int32)[None, None, :]
    named = jnp.any(match, axis=1)
    weight = jnp.sum(jnp.where(match, route_weights[:, :, None], 0.0), axis=1)
    earlier = jnp.tril(jnp.ones((tok, tok), bf16), -1)
    slot = jnp.where(named, jnp.dot(earlier, named.astype(bf16), preferred_element_type=f32), -2.0)
    place = np.arange(slots)
    spread = jnp.asarray(place[None, :] // cap == np.arange(experts)[:, None], bf16)
    wide = jnp.dot(slot.astype(bf16), spread, preferred_element_type=f32)
    chosen = wide == jnp.asarray(place % cap, f32)[None, :]
    outgoing = dot(chosen.astype(bf16), tokens, 0, 0).astype(bf16)
    arrived = exchange(outgoing.reshape(experts, cap, width), "expert")

    def by_side(array, axis):
        size = array.shape[axis] // (2 * CHIPS)
        pieces = [lax.slice_in_dim(array, k * size, (k + 1) * size, axis=axis) for k in range(2 * CHIPS)]
        even, odd = (jnp.concatenate(pieces[k::2], axis=axis) for k in range(2))
        return jnp.where(side == 0, even, odd), jnp.where(side == 0, odd, even)

    hid = routed_gate.shape[1]
    gate_up = jnp.concatenate([routed_gate[0], routed_up[0]], axis=0)
    near = [jnp.concatenate([gate_up[:, k * width : (k + 1) * width] for k in range(low, 16, 4)], axis=1) for low in range(4)]

    def columns(flip):
        low = (rank & 3) ^ flip
        return jnp.where(low < 2, jnp.where(low == 0, near[0], near[1]), jnp.where(low == 2, near[2], near[3]))

    in_mine, in_theirs = columns(0), columns(1)
    give = jnp.concatenate([columns(2), columns(3)], axis=1)
    out_mine, out_theirs = by_side(routed_down[0], 0)

    own = jnp.concatenate([shared_gate, shared_up, shared_down.T], axis=1)
    other = lax.ppermute(own, "expert", [(i, (i + ROWS) % (2 * ROWS)) for i in range(2 * ROWS)])
    pair = jnp.where(column == 0, jnp.stack([own, other]), jnp.stack([other, own]))
    across = [(i, i ^ 2) for i in range(2 * CHIPS)]
    give, late = lax.optimization_barrier((give, tokens))
    cut = give.shape[0] // 3
    far_first = lax.ppermute(give[:cut], "tensor", across)
    beside = lax.ppermute(late, "tensor", across)
    arrived, beside, pair, in_mine, in_theirs, give, far_first, out_mine, out_theirs = lax.optimization_barrier(
        (arrived, beside, pair, in_mine, in_theirs, give, far_first, out_mine, out_theirs)
    )
    far_rest = lax.ppermute(give[cut:], "tensor", across)
    gathered = lax.all_gather(pair, "expert", axis=0, axis_index_groups=LANES)

    blank = jnp.zeros((16, width), bf16)
    rows = jnp.concatenate([arrived.reshape(slots, width), tokens, blank, beside], axis=0)
    mine, theirs, far_rest = gather_halves(rows.T, RINGS, far_rest)
    far = jnp.concatenate([far_first, far_rest], axis=0)
    total = rows.shape[0]
    left, right = mine.reshape(-1, total), theirs.reshape(-1, total)
    middle = left.shape[0]
    send = dot(far[:, :middle], left, 1, 0) + dot(far[:, middle:], right, 1, 0)
    got = lax.ppermute(send[:, :slots].astype(bf16), "tensor", [(i, i ^ 2) for i in range(2 * CHIPS)])
    both = dot(in_mine, left, 1, 0) + dot(in_theirs, right, 1, 0)
    both = both[:, :slots] + got.astype(f32)
    hidden = (jax.nn.silu(both[:hid]) * both[hid:]).astype(bf16)
    hidden_mine, hidden_theirs, _ = gather_halves(hidden, SIDES)
    result = dot(hidden_mine.reshape(-1, slots), out_mine, 0, 0) + dot(
        hidden_theirs.reshape(-1, slots), out_theirs, 0, 0
    )
    result = result.astype(bf16).reshape(experts, cap, width)
    returned = exchange(result, "expert")
    partial = shared_partial(rank, mine, theirs, gathered, tok)

    def summed(parts, stride):
        total = parts[0].astype(f32)
        for k in range(1, 4):
            perm = [(i, i ^ (k * stride)) for i in range(2 * CHIPS)]
            total = total + lax.ppermute(parts[k], "tensor", perm).astype(f32)
        return total

    shared = summed(summed(partial, 4).astype(bf16), 1)

    returned, shared = lax.optimization_barrier((returned, shared))
    high = lax.reduce_precision(weight, 8, 7)
    parts = jnp.concatenate([high, weight - high], axis=0).astype(bf16)
    parts = jnp.dot(parts, spread, preferred_element_type=f32).astype(bf16).reshape(2, tok, -1)
    scaled = jnp.where(chosen[None], parts, jnp.zeros((), bf16)).reshape(2 * tok, -1)
    terms = dot(scaled, returned.reshape(slots, width), 1, 0)
    routed = terms[:tok] + terms[tok:]

    stream = (tokens.astype(f32) + shared + routed).astype(bf16)
    copies = exchange(jnp.broadcast_to(stream[None], (2 * CHIPS,) + stream.shape), "tensor")
    projected = normed_product(copies, norm_gain, proj_weight)
    return (stream, projected)


def solution(mesh):
    in_specs = (
        P("expert", "tensor"),
        P("expert", None),
        P("expert", None),
        P("expert", "tensor", None),
        P("expert", "tensor", None),
        P("expert", None, "tensor"),
        P("expert", "tensor"),
        P("expert", "tensor"),
        P("tensor", "expert"),
        P(),
        P("tensor", None),
    )
    out_specs = (P("expert", "tensor"), P("expert", "tensor"))
    return jax.shard_map(
        per_device, mesh=mesh, in_specs=in_specs, out_specs=out_specs, check_vma=False
    )
```

```python
import jax
import jax.numpy as jnp
import numpy as np
from jax import lax
from jax.experimental import pallas as pl
from jax.experimental.pallas import tpu as pltpu
from jax.sharding import PartitionSpec as P

ROWS = 16
CHIPS = 8
LANES = [[x * ROWS + z for z in range(ROWS)] for x in range(2)]
SIDES = [[2 * chip + core for chip in range(CHIPS)] for core in range(2)]
RINGS = [[4 * y + near for y in range(4)] for near in range(4)]


def dot(left, right, over_left, over_right):
    return lax.dot_general(
        left, right, (((over_left,), (over_right,)), ((), ())), preferred_element_type=jnp.float32
    )


def exchange(parts, axis, groups=None):
    return lax.all_to_all(
        parts, axis, split_axis=0, concat_axis=0, tiled=True, axis_index_groups=groups
    )


def gather_halves(block, groups, held=None):
    spread = jnp.broadcast_to(block[None], (len(groups[0]),) + block.shape)
    mine = exchange(spread, "tensor", groups)
    if held is not None:
        mine, held = lax.optimization_barrier((mine, held))
    theirs = lax.ppermute(mine, "tensor", [(i, i ^ 1) for i in range(2 * CHIPS)])
    return mine, theirs, held


def shared_kernel(rank_ref, mine_ref, far_mine_ref, theirs_ref, far_theirs_ref, table_ref, *out_refs):
    rank = rank_ref[0]
    inner = table_ref.shape[3] // 2
    size = table_ref.shape[2]
    *out_refs, hidden_ref = out_refs
    tok = out_refs[0].shape[1]

    def weights(device):
        return table_ref.at[pl.ds(2 * (device & 7), 2), device >> 3]

    def product(refs, across):
        total = jnp.zeros((mine_ref.shape[2], 2 * inner), jnp.float32)
        for y in range(4):
            for core in range(2):
                device = 4 * y + (((rank & 3) ^ (2 * across)) ^ core)
                block = weights(device)[...].reshape(2 * size, 2 * inner)
                total = total + dot(refs[core][y], block, 0, 0)
        return total

    @pl.when(pl.program_id(0) == 0)
    def _():
        sums = product((mine_ref, theirs_ref), 0)[64 : 64 + tok]
        sums = sums + product((far_mine_ref, far_theirs_ref), 1)[:tok]
        gate, up = sums[:, :inner], sums[:, inner:]
        hidden_ref[...] = (gate * (1.0 / (1.0 + jnp.exp(-gate))) * up).astype(jnp.bfloat16)

    @pl.when(pl.program_id(0) == 1)
    def _():
        hidden = hidden_ref[...]
        for near in range(4):
            for far in range(4):
                block = weights(rank ^ (near + 4 * far))[:, :, :inner].reshape(2 * size, inner)
                out_refs[far][near] = dot(hidden, block, 1, 1).astype(jnp.bfloat16)


def shared_partial(rank, mine, theirs, table, tok):
    width = mine.shape[1]
    columns = 2 * table.shape[3] // 3
    out = jax.ShapeDtypeStruct((4, tok, width), jnp.bfloat16)
    near = pl.BlockSpec((4, width, 128), lambda i: (0, 0, 4))
    far = pl.BlockSpec((4, width, 128), lambda i: (0, 0, 5))
    return pl.pallas_call(
        shared_kernel,
        out_shape=(out,) * 4,
        grid=(2,),
        in_specs=[
            pl.BlockSpec(memory_space=pltpu.SMEM),
            near,
            far,
            near,
            far,
            pl.BlockSpec(table.shape[:3] + (columns,), lambda i: (0, 0, 0, i)),
        ],
        out_specs=(pl.BlockSpec(out.shape, lambda i: (0, 0, 0)),) * 4,
        scratch_shapes=[pltpu.VMEM((tok, columns // 2), jnp.bfloat16)],
        compiler_params=pltpu.CompilerParams(vmem_limit_bytes=56 * 2**20),
        cost_estimate=pl.CostEstimate(flops=1000, bytes_accessed=1000, transcendentals=0),
    )(rank.reshape(1), mine, mine, theirs, theirs, table)


def norm_kernel(stream_ref, gain_ref, weight_ref, out_ref):
    blocks, _, width = stream_ref.shape
    squares = jnp.zeros(stream_ref.shape[1:], jnp.float32)
    for k in range(blocks):
        value = stream_ref[k].astype(jnp.float32)
        squares = squares + value * value
    mean = jnp.sum(squares, axis=1, keepdims=True) * (1.0 / (blocks * width))
    scale = lax.rsqrt(mean + 1e-06)
    total = jnp.zeros(out_ref.shape, jnp.float32)
    for k in range(0, blocks, 2):
        pair = [stream_ref[k + j].astype(jnp.float32) * scale for j in range(2)]
        pair = [(pair[j] * gain_ref[k + j : k + j + 1]).astype(jnp.bfloat16) for j in range(2)]
        total = total + dot(jnp.concatenate(pair, axis=1), weight_ref[:, k * width : (k + 2) * width], 1, 1)
    out_ref[...] = total.astype(out_ref.dtype)


def normed_product(copies, gain, weight):
    blocks, tok, width = copies.shape
    whole = pl.BlockSpec(memory_space=pltpu.VMEM)
    return pl.pallas_call(
        norm_kernel,
        out_shape=jax.ShapeDtypeStruct((tok, weight.shape[0]), jnp.bfloat16),
        in_specs=[whole, whole, whole],
        out_specs=whole,
        compiler_params=pltpu.CompilerParams(vmem_limit_bytes=24 * 2**20),
    )(copies, gain.reshape(blocks, width), weight)


def per_device(
    tokens,
    expert_ids,
    route_weights,
    routed_gate,
    routed_up,
    routed_down,
    shared_gate,
    shared_up,
    shared_down,
    norm_gain,
    proj_weight,
):
    tok, width = tokens.shape
    top = expert_ids.shape[1]
    experts = lax.axis_size("expert")
    cap = min(tok, 2 * tok * top // experts)
    slots = experts * cap
    bf16, f32 = jnp.bfloat16, jnp.float32
    rank = lax.axis_index("tensor")
    side = rank & 1
    column = lax.axis_index("expert") >> 4

    match = expert_ids[:, :, None] == jnp.arange(experts, dtype=jnp.int32)[None, None, :]
    named = jnp.any(match, axis=1)
    weight = jnp.sum(jnp.where(match, route_weights[:, :, None], 0.0), axis=1)
    earlier = jnp.tril(jnp.ones((tok, tok), bf16), -1)
    slot = jnp.where(named, jnp.dot(earlier, named.astype(bf16), preferred_element_type=f32), -2.0)
    place = np.arange(slots)
    spread = jnp.asarray(place[None, :] // cap == np.arange(experts)[:, None], bf16)
    wide = jnp.dot(slot.astype(bf16), spread, preferred_element_type=f32)
    chosen = wide == jnp.asarray(place % cap, f32)[None, :]
    outgoing = dot(chosen.astype(bf16), tokens, 0, 0).astype(bf16)
    arrived = exchange(outgoing.reshape(experts, cap, width), "expert")

    def by_side(array, axis):
        size = array.shape[axis] // (2 * CHIPS)
        pieces = [lax.slice_in_dim(array, k * size, (k + 1) * size, axis=axis) for k in range(2 * CHIPS)]
        even, odd = (jnp.concatenate(pieces[k::2], axis=axis) for k in range(2))
        return jnp.where(side == 0, even, odd), jnp.where(side == 0, odd, even)

    hid = routed_gate.shape[1]
    gate_up = jnp.concatenate([routed_gate[0], routed_up[0]], axis=0)
    near = [jnp.concatenate([gate_up[:, k * width : (k + 1) * width] for k in range(low, 16, 4)], axis=1) for low in range(4)]

    def columns(flip):
        low = (rank & 3) ^ flip
        return jnp.where(low < 2, jnp.where(low == 0, near[0], near[1]), jnp.where(low == 2, near[2], near[3]))

    in_mine, in_theirs = columns(0), columns(1)
    give = jnp.concatenate([columns(2), columns(3)], axis=1)
    out_mine, out_theirs = by_side(routed_down[0], 0)

    own = jnp.concatenate([shared_gate, shared_up, shared_down.T], axis=1)
    other = lax.ppermute(own, "expert", [(i, (i + ROWS) % (2 * ROWS)) for i in range(2 * ROWS)])
    pair = jnp.where(column == 0, jnp.stack([own, other]), jnp.stack([other, own]))
    across = [(i, i ^ 2) for i in range(2 * CHIPS)]
    give, late = lax.optimization_barrier((give, tokens))
    cut = give.shape[0] // 3
    far_first = lax.ppermute(give[:cut], "tensor", across)
    beside = lax.ppermute(late, "tensor", across)
    arrived, beside, pair, in_mine, in_theirs, give, far_first, out_mine, out_theirs = lax.optimization_barrier(
        (arrived, beside, pair, in_mine, in_theirs, give, far_first, out_mine, out_theirs)
    )
    far_rest = lax.ppermute(give[cut:], "tensor", across)
    gathered = lax.all_gather(pair, "expert", axis=0, axis_index_groups=LANES)

    blank = jnp.zeros((16, width), bf16)
    rows = jnp.concatenate([arrived.reshape(slots, width), tokens, blank, beside], axis=0)
    far = jnp.concatenate([far_first, far_rest], axis=0)
    mine, theirs, far = gather_halves(rows.T, RINGS, far)
    total = rows.shape[0]
    left, right = mine.reshape(-1, total), theirs.reshape(-1, total)
    middle = left.shape[0]
    send = dot(far[:, :middle], left, 1, 0) + dot(far[:, middle:], right, 1, 0)
    got = lax.ppermute(send[:, :slots].astype(bf16), "tensor", [(i, i ^ 2) for i in range(2 * CHIPS)])
    both = dot(in_mine, left, 1, 0) + dot(in_theirs, right, 1, 0)
    both = both[:, :slots] + got.astype(f32)
    hidden = (jax.nn.silu(both[:hid]) * both[hid:]).astype(bf16)
    hidden_mine, hidden_theirs, _ = gather_halves(hidden, SIDES)
    result = dot(hidden_mine.reshape(-1, slots), out_mine, 0, 0) + dot(
        hidden_theirs.reshape(-1, slots), out_theirs, 0, 0
    )
    result = result.astype(bf16).reshape(experts, cap, width)
    returned = exchange(result, "expert")
    partial = shared_partial(rank, mine, theirs, gathered, tok)

    def summed(parts, stride):
        total = parts[0].astype(f32)
        for k in range(1, 4):
            perm = [(i, i ^ (k * stride)) for i in range(2 * CHIPS)]
            total = total + lax.ppermute(parts[k], "tensor", perm).astype(f32)
        return total

    shared = summed(summed(partial, 4).astype(bf16), 1)

    returned, shared = lax.optimization_barrier((returned, shared))
    high = lax.reduce_precision(weight, 8, 7)
    parts = jnp.concatenate([high, weight - high], axis=0).astype(bf16)
    parts = jnp.dot(parts, spread, preferred_element_type=f32).astype(bf16).reshape(2, tok, -1)
    scaled = jnp.where(chosen[None], parts, jnp.zeros((), bf16)).reshape(2 * tok, -1)
    terms = dot(scaled, returned.reshape(slots, width), 1, 0)
    routed = terms[:tok] + terms[tok:]

    stream = (tokens.astype(f32) + shared + routed).astype(bf16)
    copies = exchange(jnp.broadcast_to(stream[None], (2 * CHIPS,) + stream.shape), "tensor")
    projected = normed_product(copies, norm_gain, proj_weight)
    return (stream, projected)


def solution(mesh):
    in_specs = (
        P("expert", "tensor"),
        P("expert", None),
        P("expert", None),
        P("expert", "tensor", None),
        P("expert", "tensor", None),
        P("expert", None, "tensor"),
        P("expert", "tensor"),
        P("expert", "tensor"),
        P("tensor", "expert"),
        P(),
        P("tensor", None),
    )
    out_specs = (P("expert", "tensor"), P("expert", "tensor"))
    return jax.shard_map(
        per_device, mesh=mesh, in_specs=in_specs, out_specs=out_specs, check_vma=False
    )
```
